32 devices in a mesh: el: 4 (over y, x), ph: 8 (over z, core).
Axes of the slice: x: 2, y: 2, z: 4, core: 2. Of those that a mesh axis runs over, the one named last changes fastest.
Arguments:
- elec_dev: float32 [128, 96, 256], P(('el', 'ph')), may hold values from -6 to 6
- phon_dev: float32 [8, 48, 96, 256], P('ph', 'el'), may hold values from -6 to 6
- elec_source: float32 [128, 96, 256], P(('el', 'ph')), may hold values from -6 to 6
- phon_source: float32 [8, 48, 96, 256], P('ph', 'el'), may hold values from -6 to 6
- elec_rate: float32 [128, 256], P(('el', 'ph')), may hold values from 0.75 to 3
- phon_rate: float32 [8, 48, 256], P('ph', 'el'), may hold values from 0.75 to 3
- tiles: bfloat16 [4, 8, 128, 256, 256], P('el', 'ph'), may hold values from -0.09375 to 0.09375
- tile_rows: int32 [4, 8, 128], P('el', 'ph'), may hold values from 0 to 31, as said below
- tile_cols: int32 [4, 8, 128], P('el', 'ph'), may hold values from 0 to 47, as said below
- tile_count: int32 [4, 8], P('el', 'ph'), may hold values from 16 to 128, as said below
Outputs:
- elec_out: float32 [128, 96, 256], P(('el', 'ph'))
- phon_out: float32 [8, 48, 96, 256], P('ph', 'el')
The draws below stay inside these ranges and needn't reach their ends.
Inputs may be any that keep to these rules, and one draw needn't show every extreme that they name: `tile_rows`: block of each slot's tile among the 32 electron blocks of its pattern row; the slots of one cell name distinct (row, column) pairs. `tile_cols`: block of each slot's tile among the 48 phonon blocks of its pattern column. Slots 0 to tile_count - 1 of a cell are live; some cell is full in every draw.
All inputs are finite; a program needn't handle non-finite values.
Results may differ from the reference program's by a relative error of at most 0.0021.
Values may be sent and summed in bfloat16 or wider, within the bound.
No kernel may reach another device: no remote copies, remote signals or barrier semaphores. Data moves between devices by JAX's collectives and lax.ppermute only.
A program may use at most 128 MiB of HBM per device.

```python
import math
import jax
import jax.numpy as jnp
from jax import lax

TILE = 256
EBLOCKS = 128
PBLOCKS = 384
TILES_DEV = 128
ITERS = 3
RHS = 96
ERB = 32
PCOL = 48
N_EL = 4
N_PH = 8


def pattern(key):
    key = jax.random.fold_in(key, 71)
    col_span = PBLOCKS // N_PH
    cell_total = EBLOCKS // N_EL * col_span
    keys = jax.random.split(key, N_EL * N_PH)
    picks = jax.vmap(lambda single: jax.random.permutation(single, cell_total)[:TILES_DEV])(keys)
    picks = picks.reshape(N_EL, N_PH, TILES_DEV).astype(jnp.int32)
    return (picks // col_span, picks % col_span)


def draw_tile_rows(key, part):
    return pattern(key)[0]


def draw_tile_cols(key, part):
    return pattern(key)[1]


def draw_tile_count(key, part):
    key = jax.random.fold_in(key, 113)
    first_key, second_key = jax.random.split(key)
    units = jax.random.randint(first_key, (N_EL * N_PH,), 0, 33).astype(jnp.int32)
    lowest = TILES_DEV // 8
    counts = lowest + (TILES_DEV - lowest) * units * units * units // 32768
    chosen = jax.random.randint(second_key, (), 0, N_EL * N_PH).astype(jnp.int32)
    counts = jnp.where(jnp.arange(N_EL * N_PH, dtype=jnp.int32) == chosen, TILES_DEV, counts)
    return counts.astype(jnp.int32).reshape(N_EL, N_PH)


def steps_of(own_key, dims, shards, least, largest):
    factor_of, own = 1.0, jax.random.fold_in(own_key, 6)
    for position, blocks in shards:
        steps = jnp.exp(jax.random.uniform(jax.random.fold_in(own, position), (blocks,), jnp.float32, least / len(shards), largest / len(shards)))
        factor_of = factor_of * jnp.repeat(steps, dims[position] // blocks).reshape([-1 if axis == position else 1 for axis in range(len(dims))])
    return factor_of


def bell_draw(stream_key, shape, spread, reach, cuts=(), kind=jnp.bfloat16):
    factor_of = steps_of(stream_key, shape, cuts, -0.22, 0.18) if cuts else 1.0
    values = jax.random.normal(stream_key, shape, jnp.float32) * spread * factor_of
    return jnp.minimum(jnp.maximum(values, -reach), reach).astype(kind)


def setup_inputs(seed: int = 0) -> dict:
    arg_keys = jax.random.split(jax.random.key(seed), 11)
    elec_dev = bell_draw(arg_keys[0], (EBLOCKS, RHS, TILE), 1.0, 6.0, ((0, 32),), jnp.float32)
    phon_dev = bell_draw(arg_keys[1], (N_PH, PCOL, RHS, TILE), 1.0, 6.0, ((0, 8), (1, 4)), jnp.float32)
    elec_source = bell_draw(arg_keys[2], (EBLOCKS, RHS, TILE), 1.0, 6.0, ((0, 32),), jnp.float32)
    phon_source = bell_draw(arg_keys[3], (N_PH, PCOL, RHS, TILE), 1.0, 6.0, ((0, 8), (1, 4)), jnp.float32)
    elec_rate = jnp.clip(jnp.exp(math.log(3.0) - 1.3862944 * jax.random.uniform(arg_keys[4], (EBLOCKS, TILE), jnp.float32) ** steps_of(arg_keys[4], (EBLOCKS, TILE), ((0, 32),), -0.2, 0.2)), 0.75, 3.0)
    phon_rate = jnp.clip(jnp.exp(math.log(3.0) - 1.3862944 * jax.random.uniform(arg_keys[5], (N_PH, PCOL, TILE), jnp.float32) ** steps_of(arg_keys[5], (N_PH, PCOL, TILE), ((0, 8), (1, 4)), -0.2, 0.2)), 0.75, 3.0)
    tiles = bell_draw(arg_keys[6], (N_EL, N_PH, TILES_DEV, TILE, TILE), (TILE * TILES_DEV * N_PH // (2 * ERB)) ** -0.5, 0.09375, ((0, 4), (1, 8)))
    tile_rows = draw_tile_rows(jax.random.fold_in(arg_keys[10], 71), 0)
    tile_cols = draw_tile_cols(jax.random.fold_in(arg_keys[10], 71), 0)
    tile_count = draw_tile_count(jax.random.fold_in(arg_keys[10], 71), 0)
    return dict(elec_dev=elec_dev, phon_dev=phon_dev, elec_source=elec_source, phon_source=phon_source, elec_rate=elec_rate, phon_rate=phon_rate, tiles=tiles, tile_rows=tile_rows, tile_cols=tile_cols, tile_count=tile_count)


def reference(elec_dev, phon_dev, elec_source, phon_source, elec_rate, phon_rate, tiles, tile_rows, tile_cols, tile_count):
    row_span = EBLOCKS // N_EL
    col_span = PBLOCKS // N_PH
    cell_count = N_EL * N_PH
    row_base = (jnp.arange(N_EL, dtype=jnp.int32) * row_span)[:, None, None]
    col_base = (jnp.arange(N_PH, dtype=jnp.int32) * col_span)[None, :, None]
    global_rows = (tile_rows + row_base).astype(jnp.int32).reshape(cell_count, TILES_DEV)
    global_cols = (tile_cols + col_base).astype(jnp.int32).reshape(cell_count, TILES_DEV)
    slot_index = jnp.arange(TILES_DEV, dtype=jnp.int32)
    active = (slot_index[None, None, :] < tile_count[:, :, None]).reshape(cell_count, TILES_DEV)
    tile_sets = tiles.reshape(cell_count, TILES_DEV, TILE, TILE)
    elec = elec_dev
    phon = phon_dev.reshape(PBLOCKS, RHS, TILE)
    phon_src = phon_source.reshape(PBLOCKS, RHS, TILE)
    elec_scale = elec_rate[:, None, :]
    phon_scale = phon_rate.reshape(PBLOCKS, TILE)[:, None, :]
    for sweep_index in range(ITERS):
        elec_half = elec.astype(jnp.bfloat16)
        phon_half = phon.astype(jnp.bfloat16)

        def one_cell(totals, inputs):
            elec_total, phon_total = totals
            tile_set, row_ids, col_ids, slot_flags = inputs
            weights = tile_set.astype(jnp.float32)
            elec_in = elec_half[row_ids].astype(jnp.float32)
            phon_in = phon_half[col_ids].astype(jnp.float32)
            slot_mask = jnp.where(slot_flags, 1.0, 0.0).astype(jnp.float32)[:, None, None]
            to_phonon = jnp.einsum("tka,tab->tkb", elec_in, weights, precision=lax.Precision.HIGHEST) * slot_mask
            to_electron = jnp.einsum("tkb,tab->tka", phon_in, weights, precision=lax.Precision.HIGHEST) * slot_mask
            return (elec_total.at[row_ids].add(to_electron), phon_total.at[col_ids].add(to_phonon)), None

        zero_totals = (jnp.zeros((EBLOCKS, RHS, TILE), jnp.float32), jnp.zeros((PBLOCKS, RHS, TILE), jnp.float32))
        drags, unused = lax.scan(one_cell, zero_totals, (tile_sets, global_rows, global_cols, active))
        elec = (elec_source + drags[0]) / elec_scale
        phon = (phon_src + drags[1]) / phon_scale
    return elec, phon.reshape(N_PH, col_span, RHS, TILE)
```

```python
import functools
import math

import jax
import jax.numpy as jnp
from jax import lax
from jax.experimental import pallas as pl
from jax.experimental.pallas import tpu as pltpu
from jax.sharding import PartitionSpec as P

ITERS = 3
DEPTH = 4
LEVELS = 32767.0
SMALLEST = 1e-33


def partner(size, step):
    if size & (size - 1) == 0:
        return lambda place: place ^ step
    return lambda place: (place + step) % size


def source_of(size, step, place):
    if size & (size - 1) == 0:
        return place ^ step
    return (place - step) % size


def send(value, axis, size, place_of):
    return lax.ppermute(value, axis, [(place, place_of(place)) for place in range(size)])


def encode(block):
    peak = jnp.maximum(jnp.max(jnp.abs(block), axis=0, keepdims=True), SMALLEST)
    coded = jnp.round(block * (LEVELS / peak)).astype(jnp.int32).astype(jnp.int16)
    return coded, peak * (1.0 / LEVELS)


def drag_body(piece_count, group, transposed, whole_outs, coded_outs, *refs):
    ids_in, ids_out, group_count, tiles = refs[:4]
    pieces = refs[4 : 4 + piece_count]
    at = 4 + piece_count
    wholes = refs[at : at + whole_outs]
    coded = refs[at + whole_outs : at + whole_outs + coded_outs]
    scales = refs[at + whole_outs + coded_outs : at + whole_outs + 2 * coded_outs]
    vectors, totals, held, piece_sems, tile_sems, out_sems = refs[at + whole_outs + 2 * coded_outs :]
    span = pieces[0].shape[0]
    loads = [
        pltpu.make_async_copy(
            pieces[index], vectors.at[pl.ds(index * span, span)], piece_sems.at[index]
        )
        for index in range(piece_count)
    ]
    for load in loads:
        load.start()
    groups = group_count[0]

    def fetch(index):
        slot = lax.rem(index, DEPTH)
        return pltpu.make_async_copy(
            tiles.at[pl.ds(index * group, group)], held.at[slot], tile_sems.at[slot]
        )

    for ahead in range(DEPTH - 1):

        @pl.when(ahead < groups)
        def _():
            fetch(ahead).start()

    totals[...] = jnp.zeros_like(totals)
    for load in loads:
        load.wait()

    def one_group(index, carry):
        @pl.when(index + DEPTH - 1 < groups)
        def _():
            fetch(index + DEPTH - 1).start()

        fetch(index).wait()
        slot = lax.rem(index, DEPTH)
        for inner in range(group):
            place = index * group + inner
            product = lax.dot_general(
                vectors[ids_in[place]],
                held[slot, inner],
                (((1,), (1 if transposed else 0,)), ((), ())),
                preferred_element_type=jnp.float32,
            )
            target = ids_out[place]
            totals[target] = totals[target] + product
        return carry

    lax.fori_loop(0, groups, one_group, 0)
    stores = []
    first = 0
    for index in range(whole_outs):
        size = wholes[index].shape[0]
        stores.append(
            pltpu.make_async_copy(
                totals.at[pl.ds(first, size)], wholes[index], out_sems.at[index]
            )
        )
        first += size
    for store in stores:
        store.start()
    for index in range(coded_outs):
        size = coded[index].shape[0]
        for block in range(size):
            coded_block, scale = encode(totals[first + block])
            coded[index][block] = coded_block
            scales[index][pl.ds(block, 1)] = scale
        first += size
    for store in stores:
        store.wait()


def drag(ids_in, ids_out, group_count, tile_set, group, pieces, transposed, whole_sizes, coded_sizes):
    span, rows, lanes = pieces[0].shape
    blocks_out = sum(whole_sizes) + sum(coded_sizes)
    any_space = pl.BlockSpec(memory_space=pl.ANY)
    smem = pl.BlockSpec(memory_space=pltpu.SMEM)
    vmem = pl.BlockSpec(memory_space=pltpu.VMEM)
    side = tile_set.shape[-1]
    return pl.pallas_call(
        functools.partial(
            drag_body, len(pieces), group, transposed, len(whole_sizes), len(coded_sizes)
        ),
        out_shape=[jax.ShapeDtypeStruct((size, rows, lanes), jnp.float32) for size in whole_sizes]
        + [jax.ShapeDtypeStruct((size, rows, lanes), jnp.int16) for size in coded_sizes]
        + [jax.ShapeDtypeStruct((size, lanes), jnp.float32) for size in coded_sizes],
        in_specs=[smem, smem, smem, any_space] + [any_space] * len(pieces),
        out_specs=[any_space] * len(whole_sizes) + [vmem] * (2 * len(coded_sizes)),
        scratch_shapes=[
            pltpu.VMEM((span * len(pieces), rows, lanes), jnp.bfloat16),
            pltpu.VMEM((blocks_out + 1, rows, lanes), jnp.float32),
            pltpu.VMEM((DEPTH, group, side, side), jnp.bfloat16),
            pltpu.SemaphoreType.DMA((len(pieces),)),
            pltpu.SemaphoreType.DMA((DEPTH,)),
            pltpu.SemaphoreType.DMA((max(len(whole_sizes), 1),)),
        ],
        compiler_params=pltpu.CompilerParams(vmem_limit_bytes=40 * 1024 * 1024),
        cost_estimate=pl.CostEstimate(
            flops=2 * tile_set.shape[0] * rows * side * side,
            bytes_accessed=tile_set.shape[0] * side * side * 2,
            transcendentals=0,
        ),
    )(ids_in, ids_out, group_count, tile_set, *pieces)


def pair_body(piece_count, mine, theirs, whole, *rest):
    coded, scales = rest[:piece_count], rest[piece_count:]
    span = whole.shape[0]
    whole[...] = mine[pl.ds(0, span)] + theirs[pl.ds(0, span)]
    for index in range(piece_count):
        for block in range(span):
            place = (index + 1) * span + block
            coded_block, scale = encode(mine[place] + theirs[place])
            coded[index][block] = coded_block
            scales[index][pl.ds(block, 1)] = scale


def pair_sum(mine, theirs, piece_count):
    blocks, rows, lanes = mine.shape
    span = blocks // (piece_count + 1)
    vmem = pl.BlockSpec(memory_space=pltpu.VMEM)
    return pl.pallas_call(
        functools.partial(pair_body, piece_count),
        out_shape=[jax.ShapeDtypeStruct((span, rows, lanes), jnp.float32)]
        + [jax.ShapeDtypeStruct((span, rows, lanes), jnp.int16)] * piece_count
        + [jax.ShapeDtypeStruct((span, lanes), jnp.float32)] * piece_count,
        in_specs=[vmem, vmem],
        out_specs=[vmem] * (1 + 2 * piece_count),
        compiler_params=pltpu.CompilerParams(vmem_limit_bytes=32 * 1024 * 1024),
    )(mine, theirs)


def renew(source, own, coded, scales, rate):
    total = own
    for values, scale in zip(coded, scales):
        total = total + values.astype(jnp.float32) * scale[:, None, :]
    return (source + total) / rate[:, None, :]


def local(
    n_el,
    n_ph,
    elec_dev,
    phon_dev,
    elec_source,
    phon_source,
    elec_rate,
    phon_rate,
    tiles,
    tile_rows,
    tile_cols,
    tile_count,
):
    tile_set = tiles[0, 0]
    slots = tile_set.shape[0]
    group = math.gcd(slots, 8)
    elec_span = elec_dev.shape[0]
    phon_span = phon_dev.shape[1]
    elec_blocks = elec_span * n_ph
    phon_blocks = phon_span * n_el
    cores = 2 if n_ph % 2 == 0 else 1
    n_z = n_ph // cores
    el_place = lax.axis_index("el")
    ph_place = lax.axis_index("ph")
    z_place, core_place = ph_place // cores, ph_place % cores

    def el_piece(owner):
        return owner ^ el_place if n_el & (n_el - 1) == 0 else (el_place - owner) % n_el

    live = jnp.arange(slots, dtype=jnp.int32) < tile_count[0, 0]
    row_ids, col_ids = tile_rows[0, 0], tile_cols[0, 0]
    col_owner = col_ids // phon_span
    row_owner = row_ids // elec_span
    row_z, row_core = row_owner // cores, row_owner % cores
    if n_el & (n_el - 1) == 0:
        phon_in = phon_out = col_owner ^ el_place
    else:
        phon_in, phon_out = (el_place - col_owner) % n_el, (col_owner - el_place) % n_el
    if n_z & (n_z - 1) == 0:
        elec_in = elec_out = row_z ^ z_place
    else:
        elec_in, elec_out = (z_place - row_z) % n_z, (row_z - z_place) % n_z
    other_core = (row_core != core_place).astype(jnp.int32)
    phon_in = phon_in * phon_span + col_ids % phon_span
    phon_out = phon_out * phon_span + col_ids % phon_span
    elec_in = (other_core * n_z + elec_in) * elec_span + row_ids % elec_span
    elec_out = (other_core * n_z + elec_out) * elec_span + row_ids % elec_span
    phon_out = jnp.where(live, phon_out, phon_blocks)
    elec_out = jnp.where(live, elec_out, elec_blocks)
    group_count = (tile_count[0] + (group - 1)) // group

    def over_el(values):
        return [
            send(value, "el", n_el, partner(n_el, step + 1)) for step, value in enumerate(values)
        ]

    def over_z(values):
        def place_of(step):
            z_of = partner(n_z, step)
            return lambda place: z_of(place // cores) * cores + place % cores

        return [send(value, "ph", n_ph, place_of(step + 1)) for step, value in enumerate(values)]

    def over_core(value):
        return send(value, "ph", n_ph, lambda place: place ^ 1)

    def spread_phon(value):
        return [value] + over_el([value] * (n_el - 1))

    def spread_elec(value):
        same_core = [value] + over_z([value] * (n_z - 1))
        if cores == 1:
            return same_core
        return same_core + [over_core(piece) for piece in same_core]

    def elec_sweep(phon_pieces):
        half = elec_blocks // cores
        halves = drag(
            phon_in, elec_out, group_count, tile_set, group, phon_pieces, True, [half] * cores, []
        )
        theirs = over_core(halves[1]) if cores == 2 else jnp.zeros_like(halves[0])
        own, *rest = pair_sum(halves[0], theirs, n_z - 1)
        coded, scales = over_z(rest[: n_z - 1]), over_z(rest[n_z - 1 :])
        return renew(elec_source, own, coded, scales, elec_rate)

    def phon_sweep(elec_pieces):
        own, *rest = drag(
            elec_in, phon_out, group_count, tile_set, group, elec_pieces, False,
            [phon_span], [phon_span] * (n_el - 1),
        )
        coded, scales = over_el(rest[: n_el - 1]), over_el(rest[n_el - 1 :])
        return renew(phon_source[0], own, coded, scales, phon_rate[0])

    elec_now, phon_now = elec_dev, phon_dev[0]
    for _ in range(ITERS):
        elec_pieces = spread_elec(elec_now.astype(jnp.bfloat16))
        phon_pieces = spread_phon(phon_now.astype(jnp.bfloat16))
        phon_now = phon_sweep(elec_pieces)
        elec_now = elec_sweep(phon_pieces)
    return (elec_now, phon_now[None])


def solution(mesh):
    in_specs = (
        P(("el", "ph"), None, None),
        P("ph", "el", None, None),
        P(("el", "ph"), None, None),
        P("ph", "el", None, None),
        P(("el", "ph"), None),
        P("ph", "el", None),
        P("el", "ph", None, None, None),
        P("el", "ph", None),
        P("el", "ph", None),
        P("el", "ph"),
    )
    out_specs = (P(("el", "ph"), None, None), P("ph", "el", None, None))
    body = functools.partial(local, mesh.shape["el"], mesh.shape["ph"])
    return jax.shard_map(body, mesh=mesh, in_specs=in_specs, out_specs=out_specs, check_vma=False)
```

```python
import functools
import math

import jax
import jax.numpy as jnp
from jax import lax
from jax.experimental import pallas as pl
from jax.experimental.pallas import tpu as pltpu
from jax.sharding import PartitionSpec as P

ITERS = 3
DEPTH = 4
COST = 1024
LEVELS = 32000.0
HIGHEST = 126.0
TAIL = 16
SMALLEST = 1e-33


def partner(size, step):
    if size & (size - 1) == 0:
        return lambda place: place ^ step
    return lambda place: (place + step) % size


def send(value, axis, size, place_of):
    return lax.ppermute(value, axis, [(place, place_of(place)) for place in range(size)])


def encode_piece(block_of, size, coded):
    rows, lanes = block_of(0).shape
    row = lax.broadcasted_iota(jnp.int32, (TAIL, lanes), 0)
    tails = [jnp.zeros((TAIL, lanes), jnp.float32) for _ in range(tail_rows(size) // TAIL)]
    for index in range(size):
        block = block_of(index)
        peak = jnp.maximum(jnp.max(jnp.abs(block), axis=0, keepdims=True), SMALLEST)
        power = jnp.minimum(jnp.floor(jnp.log2(peak)) + 1.0, HIGHEST)
        scaled = jnp.round(block * (jnp.exp2(-power) * LEVELS))
        coded[pl.ds(index * rows, rows), :] = scaled.astype(jnp.int32).astype(jnp.int16)
        tails[index // TAIL] = jnp.where(row == index % TAIL, power, tails[index // TAIL])
    for index, tail in enumerate(tails):
        coded[pl.ds(size * rows + index * TAIL, TAIL), :] = tail.astype(jnp.int32).astype(jnp.int16)


def scales_of(coded, size, rows):
    tails = [
        coded[pl.ds(size * rows + index * TAIL, TAIL), :].astype(jnp.int32).astype(jnp.float32)
        for index in range(tail_rows(size) // TAIL)
    ]
    return [
        jnp.exp2(tails[index // TAIL][index % TAIL : index % TAIL + 1]) * (1.0 / LEVELS)
        for index in range(size)
    ]


def tail_rows(size):
    return -(-size // TAIL) * TAIL


def drag_body(piece_count, group, transposed, whole_outs, coded_sizes, *refs):
    coded_outs = len(coded_sizes)
    ids_in, ids_out, group_count, tiles = refs[:4]
    pieces = refs[4 : 4 + piece_count]
    at = 4 + piece_count
    wholes = refs[at : at + whole_outs]
    coded = refs[at + whole_outs : at + whole_outs + coded_outs]
    vectors, totals, held, piece_sems, tile_sems, out_sems = refs[at + whole_outs + coded_outs :]
    span = pieces[0].shape[0]
    loads = [
        pltpu.make_async_copy(
            pieces[index], vectors.at[pl.ds(index * span, span)], piece_sems.at[index]
        )
        for index in range(piece_count)
    ]
    for load in loads:
        load.start()
    groups = group_count[0]

    def fetch(index):
        slot = lax.rem(index, DEPTH)
        return pltpu.make_async_copy(
            tiles.at[pl.ds(index * group, group)], held.at[slot], tile_sems.at[slot]
        )

    for ahead in range(DEPTH - 1):

        @pl.when(ahead < groups)
        def _():
            fetch(ahead).start()

    totals[...] = jnp.zeros_like(totals)
    for load in loads:
        load.wait()

    def one_group(index, carry):
        @pl.when(index + DEPTH - 1 < groups)
        def _():
            fetch(index + DEPTH - 1).start()

        fetch(index).wait()
        slot = lax.rem(index, DEPTH)
        for inner in range(group):
            place = index * group + inner
            product = lax.dot_general(
                vectors[ids_in[place]],
                held[slot, inner],
                (((1,), (1 if transposed else 0,)), ((), ())),
                preferred_element_type=jnp.float32,
            )
            target = ids_out[place]
            totals[target] = totals[target] + product
        return carry

    lax.fori_loop(0, groups, one_group, 0)
    stores = []
    first = 0
    for index in range(whole_outs):
        size = wholes[index].shape[0]
        stores.append(
            pltpu.make_async_copy(
                totals.at[pl.ds(first, size)], wholes[index], out_sems.at[index]
            )
        )
        first += size
    for store in stores:
        store.start()
    for index in range(coded_outs):
        size = coded_sizes[index]
        encode_piece(lambda block, first=first: totals[first + block], size, coded[index])
        first += size
    for store in stores:
        store.wait()


def coded_shape(size, rows, lanes):
    return jax.ShapeDtypeStruct((size * rows + tail_rows(size), lanes), jnp.int16)


def drag(ids_in, ids_out, group_count, tile_set, group, pieces, transposed, whole_sizes, coded_sizes):
    span, rows, lanes = pieces[0].shape
    blocks_out = sum(whole_sizes) + sum(coded_sizes)
    any_space = pl.BlockSpec(memory_space=pl.ANY)
    smem = pl.BlockSpec(memory_space=pltpu.SMEM)
    vmem = pl.BlockSpec(memory_space=pltpu.VMEM)
    side = tile_set.shape[-1]
    return pl.pallas_call(
        functools.partial(
            drag_body, len(pieces), group, transposed, len(whole_sizes), coded_sizes
        ),
        out_shape=[jax.ShapeDtypeStruct((size, rows, lanes), jnp.float32) for size in whole_sizes]
        + [coded_shape(size, rows, lanes) for size in coded_sizes],
        in_specs=[smem, smem, smem, any_space] + [any_space] * len(pieces),
        out_specs=[any_space] * len(whole_sizes) + [vmem] * len(coded_sizes),
        scratch_shapes=[
            pltpu.VMEM((span * len(pieces), rows, lanes), jnp.bfloat16),
            pltpu.VMEM((blocks_out + 1, rows, lanes), jnp.float32),
            pltpu.VMEM((DEPTH, group, side, side), jnp.bfloat16),
            pltpu.SemaphoreType.DMA((len(pieces),)),
            pltpu.SemaphoreType.DMA((DEPTH,)),
            pltpu.SemaphoreType.DMA((max(len(whole_sizes), 1),)),
        ],
        compiler_params=pltpu.CompilerParams(vmem_limit_bytes=40 * 1024 * 1024),
        cost_estimate=small_cost(),
    )(ids_in, ids_out, group_count, tile_set, *pieces)


def pair_body(mine, theirs, whole, *coded):
    span = whole.shape[0]
    whole[...] = mine[pl.ds(0, span)] + theirs[pl.ds(0, span)]
    for index, piece in enumerate(coded):
        first = (index + 1) * span
        encode_piece(lambda block, first=first: mine[first + block] + theirs[first + block], span, piece)


def pair_sum(mine, theirs, piece_count):
    blocks, rows, lanes = mine.shape
    span = blocks // (piece_count + 1)
    vmem = pl.BlockSpec(memory_space=pltpu.VMEM)
    return pl.pallas_call(
        pair_body,
        out_shape=[jax.ShapeDtypeStruct((span, rows, lanes), jnp.float32)]
        + [coded_shape(span, rows, lanes)] * piece_count,
        in_specs=[vmem, vmem],
        out_specs=[vmem] * (1 + piece_count),
        compiler_params=pltpu.CompilerParams(vmem_limit_bytes=32 * 1024 * 1024),
        cost_estimate=small_cost(),
    )(mine, theirs)


def small_cost():
    return pl.CostEstimate(flops=COST, bytes_accessed=COST, transcendentals=0)


def renew_body(source, own, rate, *refs):
    coded, result = refs[:-1], refs[-1]
    size, rows, _ = own.shape
    scales = [scales_of(piece, size, rows) for piece in coded]
    for index in range(size):
        total = own[index]
        for piece, scale in zip(coded, scales):
            values = piece[pl.ds(index * rows, rows), :].astype(jnp.int32).astype(jnp.float32)
            total = total + values * scale[index]
        fresh = (source[index] + total) / rate[pl.ds(index, 1), :]
        result[index] = fresh.astype(result.dtype)


def renew(source, own, coded, rate, dtype):
    vmem = pl.BlockSpec(memory_space=pltpu.VMEM)
    return pl.pallas_call(
        renew_body,
        out_shape=jax.ShapeDtypeStruct(own.shape, dtype),
        in_specs=[vmem] * (3 + len(coded)),
        out_specs=vmem,
        compiler_params=pltpu.CompilerParams(vmem_limit_bytes=32 * 1024 * 1024),
        cost_estimate=small_cost(),
    )(source, own, rate, *coded)


def local(
    n_el,
    n_ph,
    elec_dev,
    phon_dev,
    elec_source,
    phon_source,
    elec_rate,
    phon_rate,
    tiles,
    tile_rows,
    tile_cols,
    tile_count,
):
    tile_set = tiles[0, 0]
    slots = tile_set.shape[0]
    group = math.gcd(slots, 8)
    elec_span = elec_dev.shape[0]
    phon_span = phon_dev.shape[1]
    elec_blocks = elec_span * n_ph
    phon_blocks = phon_span * n_el
    cores = 2 if n_ph % 2 == 0 else 1
    n_z = n_ph // cores
    el_place = lax.axis_index("el")
    ph_place = lax.axis_index("ph")
    z_place, core_place = ph_place // cores, ph_place % cores

    live = jnp.arange(slots, dtype=jnp.int32) < tile_count[0, 0]
    row_ids, col_ids = tile_rows[0, 0], tile_cols[0, 0]
    col_owner = col_ids // phon_span
    row_owner = row_ids // elec_span
    row_z, row_core = row_owner // cores, row_owner % cores
    if n_el & (n_el - 1) == 0:
        phon_in = phon_out = col_owner ^ el_place
    else:
        phon_in, phon_out = (el_place - col_owner) % n_el, (col_owner - el_place) % n_el
    if n_z & (n_z - 1) == 0:
        elec_in = elec_out = row_z ^ z_place
    else:
        elec_in, elec_out = (z_place - row_z) % n_z, (row_z - z_place) % n_z
    other_core = (row_core != core_place).astype(jnp.int32)
    phon_in = phon_in * phon_span + col_ids % phon_span
    phon_out = phon_out * phon_span + col_ids % phon_span
    elec_in = (other_core * n_z + elec_in) * elec_span + row_ids % elec_span
    elec_out = (other_core * n_z + elec_out) * elec_span + row_ids % elec_span
    phon_out = jnp.where(live, phon_out, phon_blocks)
    elec_out = jnp.where(live, elec_out, elec_blocks)
    group_count = (tile_count[0] + (group - 1)) // group

    def over_el(values):
        return [
            send(value, "el", n_el, partner(n_el, step + 1)) for step, value in enumerate(values)
        ]

    def over_z(values):
        def place_of(step):
            z_of = partner(n_z, step)
            return lambda place: z_of(place // cores) * cores + place % cores

        return [send(value, "ph", n_ph, place_of(step + 1)) for step, value in enumerate(values)]

    def over_core(value):
        return send(value, "ph", n_ph, lambda place: place ^ 1)

    def spread_phon(value):
        return [value] + over_el([value] * (n_el - 1))

    def spread_elec(value):
        same_core = [value] + over_z([value] * (n_z - 1))
        if cores == 1:
            return same_core
        return same_core + [over_core(piece) for piece in same_core]

    def after(values, first):
        return list(lax.optimization_barrier((list(values), list(first)))[0])

    elec_now, phon_now = elec_dev.astype(jnp.bfloat16), phon_dev[0].astype(jnp.bfloat16)
    for sweep in range(ITERS):
        dtype = jnp.bfloat16 if sweep + 1 < ITERS else jnp.float32
        phon_pieces, elec_pieces = spread_phon(phon_now), spread_elec(elec_now)
        elec_pieces = after(elec_pieces, phon_pieces[1:3])
        phon_own, *phon_coded = drag(
            elec_in, phon_out, group_count, tile_set, group, elec_pieces, False,
            [phon_span], [phon_span] * (n_el - 1),
        )
        phon_pieces = after(phon_pieces, [phon_own])
        half = elec_blocks // cores
        halves = drag(
            phon_in, elec_out, group_count, tile_set, group, phon_pieces, True, [half] * cores, []
        )
        theirs = over_core(halves[1]) if cores == 2 else jnp.zeros_like(halves[0])
        elec_own, *elec_coded = pair_sum(halves[0], theirs, n_z - 1)
        phon_coded = over_el(phon_coded)
        elec_coded = over_z(elec_coded)
        (phon_own,) = after([phon_own], [elec_own])
        phon_now = renew(phon_source[0], phon_own, phon_coded, phon_rate[0], dtype)
        (elec_own,) = after([elec_own], [phon_now])
        elec_now = renew(elec_source, elec_own, elec_coded, elec_rate, dtype)
    return (elec_now, phon_now[None])


def solution(mesh):
    in_specs = (
        P(("el", "ph"), None, None),
        P("ph", "el", None, None),
        P(("el", "ph"), None, None),
        P("ph", "el", None, None),
        P(("el", "ph"), None),
        P("ph", "el", None),
        P("el", "ph", None, None, None),
        P("el", "ph", None),
        P("el", "ph", None),
        P("el", "ph"),
    )
    out_specs = (P(("el", "ph"), None, None), P("ph", "el", None, None))
    body = functools.partial(local, mesh.shape["el"], mesh.shape["ph"])
    return jax.shard_map(body, mesh=mesh, in_specs=in_specs, out_specs=out_specs, check_vma=False)
```

```python
import functools
import math

import jax
import jax.numpy as jnp
from jax import lax
from jax.experimental import pallas as pl
from jax.experimental.pallas import tpu as pltpu
from jax.sharding import PartitionSpec as P

ITERS = 3
DEPTH = 4
COST = 1024
LEVELS = 32000.0
HIGHEST = 126.0
TAIL = 16
TIES = 3
FORWARD = True
SMALLEST = 1e-33


def partner(size, step):
    if size & (size - 1) == 0:
        return lambda place: place ^ step
    return lambda place: (place + step) % size


def send(value, axis, size, place_of):
    return lax.ppermute(value, axis, [(place, place_of(place)) for place in range(size)])


def encode_piece(block_of, size, coded):
    rows, lanes = block_of(0).shape
    row = lax.broadcasted_iota(jnp.int32, (TAIL, lanes), 0)
    tails = [jnp.zeros((TAIL, lanes), jnp.float32) for _ in range(tail_rows(size) // TAIL)]
    for index in range(size):
        block = block_of(index)
        peak = jnp.maximum(jnp.max(jnp.abs(block), axis=0, keepdims=True), SMALLEST)
        power = jnp.minimum(jnp.floor(jnp.log2(peak)) + 1.0, HIGHEST)
        scaled = jnp.round(block * (jnp.exp2(-power) * LEVELS))
        coded[pl.ds(index * rows, rows), :] = scaled.astype(jnp.int32).astype(jnp.int16)
        tails[index // TAIL] = jnp.where(row == index % TAIL, power, tails[index // TAIL])
    for index, tail in enumerate(tails):
        coded[pl.ds(size * rows + index * TAIL, TAIL), :] = tail.astype(jnp.int32).astype(jnp.int16)


def scales_of(coded, size, rows):
    tails = [
        coded[pl.ds(size * rows + index * TAIL, TAIL), :].astype(jnp.int32).astype(jnp.float32)
        for index in range(tail_rows(size) // TAIL)
    ]
    return [
        jnp.exp2(tails[index // TAIL][index % TAIL : index % TAIL + 1]) * (1.0 / LEVELS)
        for index in range(size)
    ]


def tail_rows(size):
    return -(-size // TAIL) * TAIL


def drags_body(group, counts, *refs):
    elec_pieces, phon_pieces, elec_parts, phon_parts = counts
    elec_in, elec_out, phon_in, phon_out, group_count, tiles = refs[:6]
    refs = refs[6:]
    sources, refs = refs[: elec_pieces + phon_pieces], refs[elec_pieces + phon_pieces :]
    halves, refs = refs[:elec_parts], refs[elec_parts:]
    whole, coded, refs = refs[0], refs[1:phon_parts], refs[phon_parts:]
    elec, phon, elec_totals, phon_totals, held, source_sems, tile_sems, out_sems = refs
    loads = []
    for target, pieces in ((elec, sources[:elec_pieces]), (phon, sources[elec_pieces:])):
        first = 0
        for piece in pieces:
            span = piece.shape[0]
            loads.append(
                pltpu.make_async_copy(
                    piece, target.at[pl.ds(first, span)], source_sems.at[len(loads)]
                )
            )
            first += span
    groups = group_count[0]

    def fetch(index):
        slot = lax.rem(index, DEPTH)
        return pltpu.make_async_copy(
            tiles.at[pl.ds(index * group, group)], held.at[slot], tile_sems.at[slot]
        )

    for ahead in range(DEPTH - 1):

        @pl.when(ahead < groups)
        def _():
            fetch(ahead).start()

    for load in loads:
        load.start()
    elec_totals[...] = jnp.zeros_like(elec_totals)
    phon_totals[...] = jnp.zeros_like(phon_totals)
    for load in loads:
        load.wait()

    def one_group(index, carry):
        @pl.when(index + DEPTH - 1 < groups)
        def _():
            fetch(index + DEPTH - 1).start()

        fetch(index).wait()
        slot = lax.rem(index, DEPTH)
        for inner in range(group):
            place = index * group + inner
            tile = held[slot, inner]
            to_phon = lax.dot_general(
                elec[elec_in[place]], tile, (((1,), (0,)), ((), ())),
                preferred_element_type=jnp.float32,
            )
            to_elec = lax.dot_general(
                phon[phon_in[place]], tile, (((1,), (1,)), ((), ())),
                preferred_element_type=jnp.float32,
            )
            target = phon_out[place]
            phon_totals[target] = phon_totals[target] + to_phon
            target = elec_out[place]
            elec_totals[target] = elec_totals[target] + to_elec
        return carry

    lax.fori_loop(0, groups, one_group, 0)
    stores, first = [], 0
    for half in halves:
        size = half.shape[0]
        stores.append(
            pltpu.make_async_copy(
                elec_totals.at[pl.ds(first, size)], half, out_sems.at[len(stores)]
            )
        )
        first += size
    span = whole.shape[0]
    stores.append(
        pltpu.make_async_copy(phon_totals.at[pl.ds(0, span)], whole, out_sems.at[len(stores)])
    )
    for store in stores:
        store.start()
    for index, piece in enumerate(coded):
        first = (index + 1) * span
        encode_piece(lambda block, first=first: phon_totals[first + block], span, piece)
    for store in stores:
        store.wait()


def drags(ids, tile_set, group, elec_pieces, phon_pieces, elec_parts, phon_parts):
    _, rows, lanes = elec_pieces[0].shape
    side = tile_set.shape[-1]
    elec_blocks = sum(piece.shape[0] for piece in elec_pieces)
    phon_blocks = sum(piece.shape[0] for piece in phon_pieces)
    half, span = elec_blocks // elec_parts, phon_blocks // phon_parts
    any_space = pl.BlockSpec(memory_space=pl.ANY)
    smem = pl.BlockSpec(memory_space=pltpu.SMEM)
    vmem = pl.BlockSpec(memory_space=pltpu.VMEM)
    pieces = list(elec_pieces) + list(phon_pieces)
    outs = pl.pallas_call(
        functools.partial(
            drags_body, group, (len(elec_pieces), len(phon_pieces), elec_parts, phon_parts)
        ),
        out_shape=[jax.ShapeDtypeStruct((half, rows, lanes), jnp.float32)] * elec_parts
        + [jax.ShapeDtypeStruct((span, rows, lanes), jnp.float32)]
        + [coded_shape(span, rows, lanes)] * (phon_parts - 1),
        in_specs=[smem] * 5 + [any_space] * (1 + len(pieces)),
        out_specs=[any_space] * (elec_parts + 1) + [vmem] * (phon_parts - 1),
        scratch_shapes=[
            pltpu.VMEM((elec_blocks, rows, lanes), jnp.bfloat16),
            pltpu.VMEM((phon_blocks, rows, lanes), jnp.bfloat16),
            pltpu.VMEM((elec_blocks + 1, rows, lanes), jnp.float32),
            pltpu.VMEM((phon_blocks + 1, rows, lanes), jnp.float32),
            pltpu.VMEM((DEPTH, group, side, side), jnp.bfloat16),
            pltpu.SemaphoreType.DMA((len(pieces),)),
            pltpu.SemaphoreType.DMA((DEPTH,)),
            pltpu.SemaphoreType.DMA((elec_parts + 1,)),
        ],
        compiler_params=pltpu.CompilerParams(vmem_limit_bytes=40 * 1024 * 1024),
        cost_estimate=pl.CostEstimate(
            flops=4 * tile_set.shape[0] * rows * side * side,
            bytes_accessed=2 * tile_set.shape[0] * side * side * 2,
            transcendentals=0,
        ),
    )(*ids, tile_set, *pieces)
    return outs[:elec_parts], outs[elec_parts], outs[elec_parts + 1 :]


def coded_shape(size, rows, lanes):
    return jax.ShapeDtypeStruct((size * rows + tail_rows(size), lanes), jnp.int16)


def drag(ids_in, ids_out, group_count, tile_set, group, pieces, transposed, whole_sizes, coded_sizes):
    _, rows, lanes = pieces[0].shape
    blocks_in = sum(piece.shape[0] for piece in pieces)
    blocks_out = sum(whole_sizes) + sum(coded_sizes)
    any_space = pl.BlockSpec(memory_space=pl.ANY)
    smem = pl.BlockSpec(memory_space=pltpu.SMEM)
    vmem = pl.BlockSpec(memory_space=pltpu.VMEM)
    side = tile_set.shape[-1]
    return pl.pallas_call(
        functools.partial(
            drag_body, len(pieces), group, transposed, len(whole_sizes), coded_sizes
        ),
        out_shape=[jax.ShapeDtypeStruct((size, rows, lanes), jnp.float32) for size in whole_sizes]
        + [coded_shape(size, rows, lanes) for size in coded_sizes],
        in_specs=[smem, smem, smem, any_space] + [any_space] * len(pieces),
        out_specs=[any_space] * len(whole_sizes) + [vmem] * len(coded_sizes),
        scratch_shapes=[
            pltpu.VMEM((blocks_in, rows, lanes), jnp.bfloat16),
            pltpu.VMEM((blocks_out + 1, rows, lanes), jnp.float32),
            pltpu.VMEM((DEPTH, group, side, side), jnp.bfloat16),
            pltpu.SemaphoreType.DMA((len(pieces),)),
            pltpu.SemaphoreType.DMA((DEPTH,)),
            pltpu.SemaphoreType.DMA((max(len(whole_sizes), 1),)),
        ],
        compiler_params=pltpu.CompilerParams(vmem_limit_bytes=40 * 1024 * 1024),
        cost_estimate=pl.CostEstimate(
            flops=2 * tile_set.shape[0] * rows * side * side,
            bytes_accessed=2 * tile_set.shape[0] * side * side * 2,
            transcendentals=0,
        ),
    )(ids_in, ids_out, group_count, tile_set, *pieces)


def pair_body(mine, theirs, whole, *coded):
    span = whole.shape[0]
    whole[...] = mine[pl.ds(0, span)] + theirs[pl.ds(0, span)]
    for index, piece in enumerate(coded):
        first = (index + 1) * span
        encode_piece(lambda block, first=first: mine[first + block] + theirs[first + block], span, piece)


def pair_sum(mine, theirs, piece_count):
    blocks, rows, lanes = mine.shape
    span = blocks // (piece_count + 1)
    vmem = pl.BlockSpec(memory_space=pltpu.VMEM)
    return pl.pallas_call(
        pair_body,
        out_shape=[jax.ShapeDtypeStruct((span, rows, lanes), jnp.float32)]
        + [coded_shape(span, rows, lanes)] * piece_count,
        in_specs=[vmem, vmem],
        out_specs=[vmem] * (1 + piece_count),
        compiler_params=pltpu.CompilerParams(vmem_limit_bytes=32 * 1024 * 1024),
        cost_estimate=small_cost(),
    )(mine, theirs)


def small_cost():
    return pl.CostEstimate(flops=COST, bytes_accessed=COST, transcendentals=0)


def renew_body(source, own, rate, *refs):
    coded, result = refs[:-1], refs[-1]
    size, rows, _ = own.shape
    scales = [scales_of(piece, size, rows) for piece in coded]
    for index in range(size):
        total = own[index]
        for piece, scale in zip(coded, scales):
            values = piece[pl.ds(index * rows, rows), :].astype(jnp.int32).astype(jnp.float32)
            total = total + values * scale[index]
        fresh = (source[index] + total) / rate[pl.ds(index, 1), :]
        result[index] = fresh.astype(result.dtype)


def renew(source, own, coded, rate, dtype):
    vmem = pl.BlockSpec(memory_space=pltpu.VMEM)
    return pl.pallas_call(
        renew_body,
        out_shape=jax.ShapeDtypeStruct(own.shape, dtype),
        in_specs=[vmem] * (3 + len(coded)),
        out_specs=vmem,
        compiler_params=pltpu.CompilerParams(vmem_limit_bytes=32 * 1024 * 1024),
        cost_estimate=small_cost(),
    )(source, own, rate, *coded)


def local(
    n_el,
    n_ph,
    elec_dev,
    phon_dev,
    elec_source,
    phon_source,
    elec_rate,
    phon_rate,
    tiles,
    tile_rows,
    tile_cols,
    tile_count,
):
    tile_set = tiles[0, 0]
    slots = tile_set.shape[0]
    group = math.gcd(slots, 8)
    elec_span = elec_dev.shape[0]
    phon_span = phon_dev.shape[1]
    elec_blocks = elec_span * n_ph
    phon_blocks = phon_span * n_el
    cores = 2 if n_ph % 2 == 0 else 1
    n_z = n_ph // cores
    el_place = lax.axis_index("el")
    ph_place = lax.axis_index("ph")
    z_place, core_place = ph_place // cores, ph_place % cores

    live = jnp.arange(slots, dtype=jnp.int32) < tile_count[0, 0]
    row_ids, col_ids = tile_rows[0, 0], tile_cols[0, 0]
    col_owner = col_ids // phon_span
    row_owner = row_ids // elec_span
    row_z, row_core = row_owner // cores, row_owner % cores
    if n_el & (n_el - 1) == 0:
        phon_in = phon_out = col_owner ^ el_place
    else:
        phon_in, phon_out = (el_place - col_owner) % n_el, (col_owner - el_place) % n_el
    if n_z & (n_z - 1) == 0:
        elec_in = elec_out = row_z ^ z_place
    else:
        elec_in, elec_out = (z_place - row_z) % n_z, (row_z - z_place) % n_z
    other_core = (row_core != core_place).astype(jnp.int32)
    phon_in = phon_in * phon_span + col_ids % phon_span
    phon_out = phon_out * phon_span + col_ids % phon_span
    elec_in = (other_core * n_z + elec_in) * elec_span + row_ids % elec_span
    elec_out = (other_core * n_z + elec_out) * elec_span + row_ids % elec_span
    phon_out = jnp.where(live, phon_out, phon_blocks)
    elec_out = jnp.where(live, elec_out, elec_blocks)
    group_count = (tile_count[0] + (group - 1)) // group

    def after(values, first):
        return list(lax.optimization_barrier((list(values), list(first)))[0])

    def over_el(values):
        return [
            send(value, "el", n_el, partner(n_el, step + 1)) for step, value in enumerate(values)
        ]

    def over_z(values):
        def place_of(step):
            z_of = partner(n_z, step)
            return lambda place: z_of(place // cores) * cores + place % cores

        return [send(value, "ph", n_ph, place_of(step + 1)) for step, value in enumerate(values)]

    def over_core(value):
        return send(value, "ph", n_ph, lambda place: place ^ 1)

    def spread_phon(value):
        half = phon_span // 2
        if FORWARD and n_el == 4 and half:
            near, far = over_el([value] * 2)
            halves = after([far[:half], near[half:]], [near, far])
            passed = [
                send(piece, "el", n_el, partner(n_el, step + 1)) for step, piece in enumerate(halves)
            ]
            return [value, near, far, *passed], halves
        pieces = [value] + over_el([value] * (n_el - 1))
        return pieces, pieces[1:2]

    def spread_elec(value, first):
        same_core = [value] + over_z([value] * (n_z - 1))
        if cores == 1:
            return same_core
        others = after(same_core[1:], first)
        return same_core + [over_core(piece) for piece in [value] + others]

    ids = (elec_in, elec_out, phon_in, phon_out, group_count)
    elec_now, phon_now = elec_dev.astype(jnp.bfloat16), phon_dev[0].astype(jnp.bfloat16)
    for sweep in range(ITERS):
        dtype = jnp.bfloat16 if sweep + 1 < ITERS else jnp.float32
        phon_pieces, passed = spread_phon(phon_now)
        elec_pieces = spread_elec(elec_now, passed)
        halves, phon_own, phon_coded = drags(
            ids, tile_set, group, elec_pieces, phon_pieces, cores, n_el
        )
        theirs = over_core(halves[1]) if cores == 2 else jnp.zeros_like(halves[0])
        elec_own, *elec_coded = pair_sum(halves[0], theirs, n_z - 1)
        phon_coded, elec_coded = over_el(phon_coded), over_z(elec_coded)
        (phon_own,) = after([phon_own], [elec_own, *elec_coded[:TIES]])
        phon_now = renew(phon_source[0], phon_own, phon_coded, phon_rate[0], dtype)
        (elec_own,) = after([elec_own], [phon_now])
        elec_now = renew(elec_source, elec_own, elec_coded, elec_rate, dtype)
    return (elec_now, phon_now[None])


def solution(mesh):
    in_specs = (
        P(("el", "ph"), None, None),
        P("ph", "el", None, None),
        P(("el", "ph"), None, None),
        P("ph", "el", None, None),
        P(("el", "ph"), None),
        P("ph", "el", None),
        P("el", "ph", None, None, None),
        P("el", "ph", None),
        P("el", "ph", None),
        P("el", "ph"),
    )
    out_specs = (P(("el", "ph"), None, None), P("ph", "el", None, None))
    body = functools.partial(local, mesh.shape["el"], mesh.shape["ph"])
    return jax.shard_map(body, mesh=mesh, in_specs=in_specs, out_specs=out_specs, check_vma=False)
```

```python
import functools
import math

import jax
import jax.numpy as jnp
from jax import lax
from jax.experimental import pallas as pl
from jax.experimental.pallas import tpu as pltpu
from jax.sharding import PartitionSpec as P

ITERS = 3
DEPTH = 4
COST = 1024
LEVELS = 32000.0
HIGHEST = 126.0
TAIL = 16
TIES = 3
EARLY = 2
RELAY = True
SMALLEST = 1e-33


def partner(size, step):
    if size & (size - 1) == 0:
        return lambda place: place ^ step
    return lambda place: (place + step) % size


def send(value, axis, size, place_of):
    return lax.ppermute(value, axis, [(place, place_of(place)) for place in range(size)])


def encode_piece(block_of, size, coded):
    rows, lanes = block_of(0).shape
    row = lax.broadcasted_iota(jnp.int32, (TAIL, lanes), 0)
    tails = [jnp.zeros((TAIL, lanes), jnp.float32) for _ in range(tail_rows(size) // TAIL)]
    for index in range(size):
        block = block_of(index)
        peak = jnp.maximum(jnp.max(jnp.abs(block), axis=0, keepdims=True), SMALLEST)
        power = jnp.minimum(jnp.floor(jnp.log2(peak)) + 1.0, HIGHEST)
        scaled = jnp.round(block * (jnp.exp2(-power) * LEVELS))
        coded[pl.ds(index * rows, rows), :] = scaled.astype(jnp.int32).astype(jnp.int16)
        tails[index // TAIL] = jnp.where(row == index % TAIL, power, tails[index // TAIL])
    for index, tail in enumerate(tails):
        coded[pl.ds(size * rows + index * TAIL, TAIL), :] = tail.astype(jnp.int32).astype(jnp.int16)


def scales_of(coded, size, rows):
    tails = [
        coded[pl.ds(size * rows + index * TAIL, TAIL), :].astype(jnp.int32).astype(jnp.float32)
        for index in range(tail_rows(size) // TAIL)
    ]
    return [
        jnp.exp2(tails[index // TAIL][index % TAIL : index % TAIL + 1]) * (1.0 / LEVELS)
        for index in range(size)
    ]


def tail_rows(size):
    return -(-size // TAIL) * TAIL


def drags_body(group, counts, kept, *refs):
    elec_pieces, phon_pieces = counts
    elec_kept, phon_kept, plan = kept
    elec_in, elec_out, phon_in, phon_out, group_count, tiles = refs[:6]
    refs = refs[6:]
    sources, refs = refs[: elec_pieces + phon_pieces], refs[elec_pieces + phon_pieces :]
    whole, refs = refs[: len(elec_kept) + len(phon_kept)], refs[len(elec_kept) + len(phon_kept) :]
    coded, refs = refs[: len(plan)], refs[len(plan) :]
    elec, phon, elec_totals, phon_totals, held, source_sems, tile_sems, out_sems = refs
    loads = []
    for target, pieces in ((elec, sources[:elec_pieces]), (phon, sources[elec_pieces:])):
        first = 0
        for piece in pieces:
            span = piece.shape[0]
            loads.append(
                pltpu.make_async_copy(
                    piece, target.at[pl.ds(first, span)], source_sems.at[len(loads)]
                )
            )
            first += span
    groups = group_count[0]

    def fetch(index):
        slot = lax.rem(index, DEPTH)
        return pltpu.make_async_copy(
            tiles.at[pl.ds(index * group, group)], held.at[slot], tile_sems.at[slot]
        )

    for ahead in range(DEPTH - 1):

        @pl.when(ahead < groups)
        def _():
            fetch(ahead).start()

    for load in loads:
        load.start()
    elec_totals[...] = jnp.zeros_like(elec_totals)
    phon_totals[...] = jnp.zeros_like(phon_totals)
    for load in loads:
        load.wait()

    def one_group(index, carry):
        @pl.when(index + DEPTH - 1 < groups)
        def _():
            fetch(index + DEPTH - 1).start()

        fetch(index).wait()
        slot = lax.rem(index, DEPTH)
        for inner in range(group):
            place = index * group + inner
            tile = held[slot, inner]
            to_phon = lax.dot_general(
                elec[elec_in[place]], tile, (((1,), (0,)), ((), ())),
                preferred_element_type=jnp.float32,
            )
            to_elec = lax.dot_general(
                phon[phon_in[place]], tile, (((1,), (1,)), ((), ())),
                preferred_element_type=jnp.float32,
            )
            target = phon_out[place]
            phon_totals[target] = phon_totals[target] + to_phon
            target = elec_out[place]
            elec_totals[target] = elec_totals[target] + to_elec
        return carry

    lax.fori_loop(0, groups, one_group, 0)
    places = [(elec_totals, span) for span in elec_kept] + [(phon_totals, span) for span in phon_kept]
    stores = [
        pltpu.make_async_copy(
            totals.at[pl.ds(first, end - first)], whole[index], out_sems.at[index]
        )
        for index, (totals, (first, end)) in enumerate(places)
    ]
    for store in stores:
        store.start()
    for blocks, piece in zip(plan, coded):
        encode_piece(lambda index, blocks=blocks: phon_totals[blocks[index]], len(blocks), piece)
    for store in stores:
        store.wait()


def drags(ids, tile_set, group, elec_pieces, phon_pieces, kept):
    elec_kept, phon_kept, plan = kept
    _, rows, lanes = elec_pieces[0].shape
    side = tile_set.shape[-1]
    elec_blocks = sum(piece.shape[0] for piece in elec_pieces)
    phon_blocks = sum(piece.shape[0] for piece in phon_pieces)
    any_space = pl.BlockSpec(memory_space=pl.ANY)
    smem = pl.BlockSpec(memory_space=pltpu.SMEM)
    vmem = pl.BlockSpec(memory_space=pltpu.VMEM)
    pieces = list(elec_pieces) + list(phon_pieces)
    whole = list(elec_kept) + list(phon_kept)
    outs = pl.pallas_call(
        functools.partial(drags_body, group, (len(elec_pieces), len(phon_pieces)), kept),
        out_shape=[
            jax.ShapeDtypeStruct((end - first, rows, lanes), jnp.float32) for first, end in whole
        ]
        + [coded_shape(len(blocks), rows, lanes) for blocks in plan],
        in_specs=[smem] * 5 + [any_space] * (1 + len(pieces)),
        out_specs=[any_space] * len(whole) + [vmem] * len(plan),
        scratch_shapes=[
            pltpu.VMEM((elec_blocks, rows, lanes), jnp.bfloat16),
            pltpu.VMEM((phon_blocks, rows, lanes), jnp.bfloat16),
            pltpu.VMEM((elec_blocks + 1, rows, lanes), jnp.float32),
            pltpu.VMEM((phon_blocks + 1, rows, lanes), jnp.float32),
            pltpu.VMEM((DEPTH, group, side, side), jnp.bfloat16),
            pltpu.SemaphoreType.DMA((len(pieces),)),
            pltpu.SemaphoreType.DMA((DEPTH,)),
            pltpu.SemaphoreType.DMA((len(whole),)),
        ],
        compiler_params=pltpu.CompilerParams(vmem_limit_bytes=40 * 1024 * 1024),
        cost_estimate=pl.CostEstimate(
            flops=4 * tile_set.shape[0] * rows * side * side,
            bytes_accessed=2 * tile_set.shape[0] * side * side * 2,
            transcendentals=0,
        ),
    )(*ids, tile_set, *pieces)
    return outs[: len(elec_kept)], outs[len(elec_kept) : len(whole)], outs[len(whole) :]


def coded_shape(size, rows, lanes):
    return jax.ShapeDtypeStruct((size * rows + tail_rows(size), lanes), jnp.int16)


def drag(ids_in, ids_out, group_count, tile_set, group, pieces, transposed, whole_sizes, coded_sizes):
    _, rows, lanes = pieces[0].shape
    blocks_in = sum(piece.shape[0] for piece in pieces)
    blocks_out = sum(whole_sizes) + sum(coded_sizes)
    any_space = pl.BlockSpec(memory_space=pl.ANY)
    smem = pl.BlockSpec(memory_space=pltpu.SMEM)
    vmem = pl.BlockSpec(memory_space=pltpu.VMEM)
    side = tile_set.shape[-1]
    return pl.pallas_call(
        functools.partial(
            drag_body, len(pieces), group, transposed, len(whole_sizes), coded_sizes
        ),
        out_shape=[jax.ShapeDtypeStruct((size, rows, lanes), jnp.float32) for size in whole_sizes]
        + [coded_shape(size, rows, lanes) for size in coded_sizes],
        in_specs=[smem, smem, smem, any_space] + [any_space] * len(pieces),
        out_specs=[any_space] * len(whole_sizes) + [vmem] * len(coded_sizes),
        scratch_shapes=[
            pltpu.VMEM((blocks_in, rows, lanes), jnp.bfloat16),
            pltpu.VMEM((blocks_out + 1, rows, lanes), jnp.float32),
            pltpu.VMEM((DEPTH, group, side, side), jnp.bfloat16),
            pltpu.SemaphoreType.DMA((len(pieces),)),
            pltpu.SemaphoreType.DMA((DEPTH,)),
            pltpu.SemaphoreType.DMA((max(len(whole_sizes), 1),)),
        ],
        compiler_params=pltpu.CompilerParams(vmem_limit_bytes=40 * 1024 * 1024),
        cost_estimate=pl.CostEstimate(
            flops=2 * tile_set.shape[0] * rows * side * side,
            bytes_accessed=2 * tile_set.shape[0] * side * side * 2,
            transcendentals=0,
        ),
    )(ids_in, ids_out, group_count, tile_set, *pieces)


def pair_body(mine, theirs, whole, *coded):
    span = whole.shape[0]
    whole[...] = mine[pl.ds(0, span)] + theirs[pl.ds(0, span)]
    for index, piece in enumerate(coded):
        first = (index + 1) * span
        encode_piece(lambda block, first=first: mine[first + block] + theirs[first + block], span, piece)


def pair_sum(mine, theirs, piece_count):
    blocks, rows, lanes = theirs.shape
    span = blocks // (piece_count + 1)
    vmem = pl.BlockSpec(memory_space=pltpu.VMEM)
    return pl.pallas_call(
        pair_body,
        out_shape=[jax.ShapeDtypeStruct((span, rows, lanes), jnp.float32)]
        + [coded_shape(span, rows, lanes)] * piece_count,
        in_specs=[vmem, vmem],
        out_specs=[vmem] * (1 + piece_count),
        compiler_params=pltpu.CompilerParams(vmem_limit_bytes=32 * 1024 * 1024),
        cost_estimate=small_cost(),
    )(mine, theirs)


def small_cost():
    return pl.CostEstimate(flops=COST, bytes_accessed=COST, transcendentals=0)


def decode(piece, index, scales, rows):
    values = piece[pl.ds(index * rows, rows), :].astype(jnp.int32).astype(jnp.float32)
    return values * scales[index]


def piece_size(piece, rows):
    return next(size for size in range(piece.shape[0] // rows + 1) if size * rows + tail_rows(size) == piece.shape[0])


def renew_body(terms, source, own, rate, *refs):
    coded, result = refs[:-1], refs[-1]
    _, rows, _ = result.shape
    scales = [scales_of(piece, piece_size(piece, rows), rows) for piece in coded]
    for index, parts in enumerate(terms):
        total = own[index]
        for piece, place in parts:
            total = total + decode(coded[piece], place, scales[piece], rows)
        fresh = (source[index] + total) / rate[pl.ds(index, 1), :]
        result[index] = fresh.astype(result.dtype)


def renew(source, own, coded, terms, rate, dtype):
    vmem = pl.BlockSpec(memory_space=pltpu.VMEM)
    return pl.pallas_call(
        functools.partial(renew_body, terms),
        out_shape=jax.ShapeDtypeStruct(source.shape, dtype),
        in_specs=[vmem] * (3 + len(coded)),
        out_specs=vmem,
        compiler_params=pltpu.CompilerParams(vmem_limit_bytes=32 * 1024 * 1024),
        cost_estimate=small_cost(),
    )(source, own, rate, *coded)


def combine_body(plan, totals, *refs):
    taken, given = refs[: len(plan)], refs[len(plan) :]
    _, rows, _ = totals.shape
    for blocks, source, target in zip(plan, taken, given):
        scales = scales_of(source, piece_size(source, rows), rows)
        encode_piece(
            lambda index, blocks=blocks, source=source, scales=scales: totals[blocks[index]]
            + decode(source, index, scales, rows),
            len(blocks), target,
        )


def combine(totals, taken, plan):
    _, rows, lanes = totals.shape
    vmem = pl.BlockSpec(memory_space=pltpu.VMEM)
    return pl.pallas_call(
        functools.partial(combine_body, plan),
        out_shape=[coded_shape(len(blocks), rows, lanes) for blocks in plan],
        in_specs=[vmem] * (1 + len(taken)),
        out_specs=[vmem] * len(plan),
        compiler_params=pltpu.CompilerParams(vmem_limit_bytes=32 * 1024 * 1024),
        cost_estimate=small_cost(),
    )(totals, *taken)


def local(
    n_el,
    n_ph,
    elec_dev,
    phon_dev,
    elec_source,
    phon_source,
    elec_rate,
    phon_rate,
    tiles,
    tile_rows,
    tile_cols,
    tile_count,
):
    tile_set = tiles[0, 0]
    slots = tile_set.shape[0]
    group = math.gcd(slots, 8)
    elec_span = elec_dev.shape[0]
    phon_span = phon_dev.shape[1]
    elec_blocks = elec_span * n_ph
    phon_blocks = phon_span * n_el
    cores = 2 if n_ph % 2 == 0 else 1
    n_z = n_ph // cores
    el_place = lax.axis_index("el")
    ph_place = lax.axis_index("ph")
    z_place, core_place = ph_place // cores, ph_place % cores

    live = jnp.arange(slots, dtype=jnp.int32) < tile_count[0, 0]
    row_ids, col_ids = tile_rows[0, 0], tile_cols[0, 0]
    col_owner = col_ids // phon_span
    row_owner = row_ids // elec_span
    row_z, row_core = row_owner // cores, row_owner % cores
    if n_el & (n_el - 1) == 0:
        phon_in = phon_out = col_owner ^ el_place
    else:
        phon_in, phon_out = (el_place - col_owner) % n_el, (col_owner - el_place) % n_el
    if n_z & (n_z - 1) == 0:
        elec_in = elec_out = row_z ^ z_place
    else:
        elec_in, elec_out = (z_place - row_z) % n_z, (row_z - z_place) % n_z
    other_core = (row_core != core_place).astype(jnp.int32)
    phon_in = phon_in * phon_span + col_ids % phon_span
    phon_out = phon_out * phon_span + col_ids % phon_span
    elec_in = (other_core * n_z + elec_in) * elec_span + row_ids % elec_span
    elec_out = (other_core * n_z + elec_out) * elec_span + row_ids % elec_span
    phon_out = jnp.where(live, phon_out, phon_blocks)
    elec_out = jnp.where(live, elec_out, elec_blocks)
    group_count = (tile_count[0] + (group - 1)) // group

    def after(values, first):
        return list(lax.optimization_barrier((list(values), list(first)))[0])

    def over_el(values):
        return [
            send(value, "el", n_el, partner(n_el, step + 1)) for step, value in enumerate(values)
        ]

    def over_z(values):
        def place_of(step):
            z_of = partner(n_z, step)
            return lambda place: z_of(place // cores) * cores + place % cores

        return [send(value, "ph", n_ph, place_of(step + 1)) for step, value in enumerate(values)]

    def over_core(value):
        return send(value, "ph", n_ph, lambda place: place ^ 1)

    def spread_phon(value):
        half = phon_span // 2
        if RELAY and n_el == 4 and half:
            near, far = over_el([value] * 2)
            halves = after([far[:half], near[half:]], [near, far])
            passed = [
                send(piece, "el", n_el, partner(n_el, step + 1)) for step, piece in enumerate(halves)
            ]
            return [value, near, far, *passed], halves
        pieces = [value] + over_el([value] * (n_el - 1))
        return pieces, pieces[1:2]

    def spread_elec(value, first):
        same_core = [value] + over_z([value] * (n_z - 1))
        if cores == 1:
            return same_core
        others = after(same_core[1:], first)
        return same_core + [over_core(piece) for piece in [value] + others]

    elec_terms = [[(step, index) for step in range(n_z - 1)] for index in range(elec_span)]
    half = phon_span // 2
    relay = RELAY and n_el == 4 and phon_span % 2 == 0
    near, far, both = phon_span, 2 * phon_span, 3 * phon_span
    if relay:
        plan = [
            [start + index for start in (both, near) for index in range(half)],
            [start + index for start in (both, far) for index in range(half, phon_span)],
        ]
        combined = [list(range(half)), list(range(half, phon_span))]
        phon_terms = [[(0, half + index), (3, index)] for index in range(half)]
        phon_terms += [[(1, half + index), (2, index)] for index in range(half)]
    else:
        plan = [
            list(range((step + 1) * phon_span, (step + 2) * phon_span)) for step in range(n_el - 1)
        ]
        phon_terms = [[(step, index) for step in range(n_el - 1)] for index in range(phon_span)]
    middle = elec_blocks // 2
    kept = (
        [(0, middle), (middle, elec_blocks)],
        [(0, phon_span)] + [(near + half, far + half)] * relay,
        plan,
    )
    ids = (elec_in, elec_out, phon_in, phon_out, group_count)
    elec_now, phon_now = elec_dev.astype(jnp.bfloat16), phon_dev[0].astype(jnp.bfloat16)
    for sweep in range(ITERS):
        dtype = jnp.bfloat16 if sweep + 1 < ITERS else jnp.float32
        phon_pieces, passed = spread_phon(phon_now)
        elec_pieces = spread_elec(elec_now, passed)
        (elec_own, given), phon_own, phon_coded = drags(
            ids, tile_set, group, elec_pieces, phon_pieces, kept
        )
        theirs = over_core(given)
        elec_own, *elec_coded = pair_sum(elec_own, theirs, n_z - 1)
        elec_coded = over_z(elec_coded)
        phon_coded = over_el(phon_coded)
        if relay:
            taken = after(phon_coded[::-1], [elec_own, *elec_coded[:EARLY]])
            phon_coded += over_el(combine(phon_own[1], taken, combined))
        (phon_kept,) = after(phon_own[:1], [elec_own, *elec_coded[:TIES]])
        phon_now = renew(phon_source[0], phon_kept, phon_coded, phon_terms, phon_rate[0], dtype)
        (elec_own,) = after([elec_own], [phon_now])
        elec_now = renew(elec_source, elec_own, elec_coded, elec_terms, elec_rate, dtype)
    return (elec_now, phon_now[None])


def solution(mesh):
    in_specs = (
        P(("el", "ph"), None, None),
        P("ph", "el", None, None),
        P(("el", "ph"), None, None),
        P("ph", "el", None, None),
        P(("el", "ph"), None),
        P("ph", "el", None),
        P("el", "ph", None, None, None),
        P("el", "ph", None),
        P("el", "ph", None),
        P("el", "ph"),
    )
    out_specs = (P(("el", "ph"), None, None), P("ph", "el", None, None))
    body = functools.partial(local, mesh.shape["el"], mesh.shape["ph"])
    return jax.shard_map(body, mesh=mesh, in_specs=in_specs, out_specs=out_specs, check_vma=False)
```

```python
import functools
import math

import jax
import jax.numpy as jnp
from jax import lax
from jax.experimental import pallas as pl
from jax.experimental.pallas import tpu as pltpu
from jax.sharding import PartitionSpec as P

ITERS = 3
DEPTH = 3
COST = 1024
LEVELS = 32000.0
HIGHEST = 126.0
TAIL = 16
TIES = 3
EARLY = 2
RELAY = True
SMALLEST = 1e-33


def partner(size, step):
    if size & (size - 1) == 0:
        return lambda place: place ^ step
    return lambda place: (place + step) % size


def send(value, axis, size, place_of):
    return lax.ppermute(value, axis, [(place, place_of(place)) for place in range(size)])


def encode_piece(block_of, size, coded):
    rows, lanes = block_of(0).shape
    row = lax.broadcasted_iota(jnp.int32, (TAIL, lanes), 0)
    tails = [jnp.zeros((TAIL, lanes), jnp.float32) for _ in range(tail_rows(size) // TAIL)]
    for index in range(size):
        block = block_of(index)
        peak = jnp.maximum(jnp.max(jnp.abs(block), axis=0, keepdims=True), SMALLEST)
        power = jnp.minimum(jnp.floor(jnp.log2(peak)) + 1.0, HIGHEST)
        scaled = jnp.round(block * (jnp.exp2(-power) * LEVELS))
        coded[pl.ds(index * rows, rows), :] = scaled.astype(jnp.int32).astype(jnp.int16)
        tails[index // TAIL] = jnp.where(row == index % TAIL, power, tails[index // TAIL])
    for index, tail in enumerate(tails):
        coded[pl.ds(size * rows + index * TAIL, TAIL), :] = tail.astype(jnp.int32).astype(jnp.int16)


def scales_of(coded, size, rows):
    tails = [
        coded[pl.ds(size * rows + index * TAIL, TAIL), :].astype(jnp.int32).astype(jnp.float32)
        for index in range(tail_rows(size) // TAIL)
    ]
    return [
        jnp.exp2(tails[index // TAIL][index % TAIL : index % TAIL + 1]) * (1.0 / LEVELS)
        for index in range(size)
    ]


def tail_rows(size):
    return -(-size // TAIL) * TAIL


def drags_body(group, counts, kept, *refs):
    elec_pieces, phon_pieces = counts
    elec_kept, phon_kept, plan = kept
    elec_in, elec_out, phon_in, phon_out, group_count, tiles = refs[:6]
    refs = refs[6:]
    sources, refs = refs[: elec_pieces + phon_pieces], refs[elec_pieces + phon_pieces :]
    whole, refs = refs[: len(elec_kept) + len(phon_kept)], refs[len(elec_kept) + len(phon_kept) :]
    coded, refs = refs[: len(plan)], refs[len(plan) :]
    elec, phon, elec_totals, phon_totals, held, tile_sems, out_sems = refs
    groups = group_count[0]

    def fetch(index):
        slot = lax.rem(index, DEPTH)
        return pltpu.make_async_copy(
            tiles.at[pl.ds(index * group, group)], held.at[slot], tile_sems.at[slot]
        )

    for ahead in range(DEPTH - 1):

        @pl.when(ahead < groups)
        def _():
            fetch(ahead).start()

    for target, pieces in ((elec, sources[:elec_pieces]), (phon, sources[elec_pieces:])):
        first = 0
        for piece in pieces:
            span = piece.shape[0]
            target[pl.ds(first, span)] = piece[...]
            first += span
    elec_totals[...] = jnp.zeros_like(elec_totals)
    phon_totals[...] = jnp.zeros_like(phon_totals)

    def one_group(index, carry):
        @pl.when(index + DEPTH - 1 < groups)
        def _():
            fetch(index + DEPTH - 1).start()

        fetch(index).wait()
        slot = lax.rem(index, DEPTH)
        for inner in range(group):
            place = index * group + inner
            tile = held[slot, inner]
            to_phon = lax.dot_general(
                elec[elec_in[place]], tile, (((1,), (0,)), ((), ())),
                preferred_element_type=jnp.float32,
            )
            to_elec = lax.dot_general(
                phon[phon_in[place]], tile, (((1,), (1,)), ((), ())),
                preferred_element_type=jnp.float32,
            )
            target = phon_out[place]
            phon_totals[target] = phon_totals[target] + to_phon
            target = elec_out[place]
            elec_totals[target] = elec_totals[target] + to_elec
        return carry

    lax.fori_loop(0, groups, one_group, 0)
    places = [(elec_totals, span) for span in elec_kept] + [(phon_totals, span) for span in phon_kept]
    stores = [
        pltpu.make_async_copy(
            totals.at[pl.ds(first, end - first)], whole[index], out_sems.at[index]
        )
        for index, (totals, (first, end)) in enumerate(places)
    ]
    for store in stores:
        store.start()
    for blocks, piece in zip(plan, coded):
        encode_piece(lambda index, blocks=blocks: phon_totals[blocks[index]], len(blocks), piece)
    for store in stores:
        store.wait()


def drags(ids, tile_set, group, elec_pieces, phon_pieces, kept):
    elec_kept, phon_kept, plan = kept
    _, rows, lanes = elec_pieces[0].shape
    side = tile_set.shape[-1]
    elec_blocks = sum(piece.shape[0] for piece in elec_pieces)
    phon_blocks = sum(piece.shape[0] for piece in phon_pieces)
    any_space = pl.BlockSpec(memory_space=pl.ANY)
    smem = pl.BlockSpec(memory_space=pltpu.SMEM)
    vmem = pl.BlockSpec(memory_space=pltpu.VMEM)
    pieces = list(elec_pieces) + list(phon_pieces)
    whole = list(elec_kept) + list(phon_kept)
    outs = pl.pallas_call(
        functools.partial(drags_body, group, (len(elec_pieces), len(phon_pieces)), kept),
        out_shape=[
            jax.ShapeDtypeStruct((end - first, rows, lanes), jnp.float32) for first, end in whole
        ]
        + [coded_shape(len(blocks), rows, lanes) for blocks in plan],
        in_specs=[smem] * 5 + [any_space] + [vmem] * len(pieces),
        out_specs=[any_space] * len(whole) + [vmem] * len(plan),
        scratch_shapes=[
            pltpu.VMEM((elec_blocks, rows, lanes), jnp.bfloat16),
            pltpu.VMEM((phon_blocks, rows, lanes), jnp.bfloat16),
            pltpu.VMEM((elec_blocks + 1, rows, lanes), jnp.float32),
            pltpu.VMEM((phon_blocks + 1, rows, lanes), jnp.float32),
            pltpu.VMEM((DEPTH, group, side, side), jnp.bfloat16),
            pltpu.SemaphoreType.DMA((DEPTH,)),
            pltpu.SemaphoreType.DMA((len(whole),)),
        ],
        compiler_params=pltpu.CompilerParams(vmem_limit_bytes=40 * 1024 * 1024),
        cost_estimate=pl.CostEstimate(
            flops=4 * tile_set.shape[0] * rows * side * side,
            bytes_accessed=2 * tile_set.shape[0] * side * side * 2,
            transcendentals=0,
        ),
    )(*ids, tile_set, *pieces)
    return outs[: len(elec_kept)], outs[len(elec_kept) : len(whole)], outs[len(whole) :]


def coded_shape(size, rows, lanes):
    return jax.ShapeDtypeStruct((size * rows + tail_rows(size), lanes), jnp.int16)


def drag(ids_in, ids_out, group_count, tile_set, group, pieces, transposed, whole_sizes, coded_sizes):
    _, rows, lanes = pieces[0].shape
    blocks_in = sum(piece.shape[0] for piece in pieces)
    blocks_out = sum(whole_sizes) + sum(coded_sizes)
    any_space = pl.BlockSpec(memory_space=pl.ANY)
    smem = pl.BlockSpec(memory_space=pltpu.SMEM)
    vmem = pl.BlockSpec(memory_space=pltpu.VMEM)
    side = tile_set.shape[-1]
    return pl.pallas_call(
        functools.partial(
            drag_body, len(pieces), group, transposed, len(whole_sizes), coded_sizes
        ),
        out_shape=[jax.ShapeDtypeStruct((size, rows, lanes), jnp.float32) for size in whole_sizes]
        + [coded_shape(size, rows, lanes) for size in coded_sizes],
        in_specs=[smem, smem, smem, any_space] + [any_space] * len(pieces),
        out_specs=[any_space] * len(whole_sizes) + [vmem] * len(coded_sizes),
        scratch_shapes=[
            pltpu.VMEM((blocks_in, rows, lanes), jnp.bfloat16),
            pltpu.VMEM((blocks_out + 1, rows, lanes), jnp.float32),
            pltpu.VMEM((DEPTH, group, side, side), jnp.bfloat16),
            pltpu.SemaphoreType.DMA((DEPTH,)),
            pltpu.SemaphoreType.DMA((max(len(whole_sizes), 1),)),
        ],
        compiler_params=pltpu.CompilerParams(vmem_limit_bytes=40 * 1024 * 1024),
        cost_estimate=pl.CostEstimate(
            flops=2 * tile_set.shape[0] * rows * side * side,
            bytes_accessed=2 * tile_set.shape[0] * side * side * 2,
            transcendentals=0,
        ),
    )(ids_in, ids_out, group_count, tile_set, *pieces)


def pair_body(mine, theirs, whole, *coded):
    span = whole.shape[0]
    whole[...] = mine[pl.ds(0, span)] + theirs[pl.ds(0, span)]
    for index, piece in enumerate(coded):
        first = (index + 1) * span
        encode_piece(lambda block, first=first: mine[first + block] + theirs[first + block], span, piece)


def pair_sum(mine, theirs, piece_count):
    blocks, rows, lanes = theirs.shape
    span = blocks // (piece_count + 1)
    vmem = pl.BlockSpec(memory_space=pltpu.VMEM)
    return pl.pallas_call(
        pair_body,
        out_shape=[jax.ShapeDtypeStruct((span, rows, lanes), jnp.float32)]
        + [coded_shape(span, rows, lanes)] * piece_count,
        in_specs=[vmem, vmem],
        out_specs=[vmem] * (1 + piece_count),
        compiler_params=pltpu.CompilerParams(vmem_limit_bytes=32 * 1024 * 1024),
        cost_estimate=small_cost(),
    )(mine, theirs)


def small_cost():
    return pl.CostEstimate(flops=COST, bytes_accessed=COST, transcendentals=0)


def decode(piece, index, scales, rows):
    values = piece[pl.ds(index * rows, rows), :].astype(jnp.int32).astype(jnp.float32)
    return values * scales[index]


def piece_size(piece, rows):
    return next(size for size in range(piece.shape[0] // rows + 1) if size * rows + tail_rows(size) == piece.shape[0])


def renew_body(terms, source, own, rate, *refs):
    coded, result = refs[:-1], refs[-1]
    _, rows, _ = result.shape
    scales = [scales_of(piece, piece_size(piece, rows), rows) for piece in coded]
    for index, parts in enumerate(terms):
        total = own[index]
        for piece, place in parts:
            total = total + decode(coded[piece], place, scales[piece], rows)
        fresh = (source[index] + total) / rate[pl.ds(index, 1), :]
        result[index] = fresh.astype(result.dtype)


def renew(source, own, coded, terms, rate, dtype):
    vmem = pl.BlockSpec(memory_space=pltpu.VMEM)
    return pl.pallas_call(
        functools.partial(renew_body, terms),
        out_shape=jax.ShapeDtypeStruct(source.shape, dtype),
        in_specs=[vmem] * (3 + len(coded)),
        out_specs=vmem,
        compiler_params=pltpu.CompilerParams(vmem_limit_bytes=32 * 1024 * 1024),
        cost_estimate=small_cost(),
    )(source, own, rate, *coded)


def combine_body(plan, totals, *refs):
    taken, given = refs[: len(plan)], refs[len(plan) :]
    _, rows, _ = totals.shape
    for blocks, source, target in zip(plan, taken, given):
        scales = scales_of(source, piece_size(source, rows), rows)
        encode_piece(
            lambda index, blocks=blocks, source=source, scales=scales: totals[blocks[index]]
            + decode(source, index, scales, rows),
            len(blocks), target,
        )


def combine(totals, taken, plan):
    _, rows, lanes = totals.shape
    vmem = pl.BlockSpec(memory_space=pltpu.VMEM)
    return pl.pallas_call(
        functools.partial(combine_body, plan),
        out_shape=[coded_shape(len(blocks), rows, lanes) for blocks in plan],
        in_specs=[vmem] * (1 + len(taken)),
        out_specs=[vmem] * len(plan),
        compiler_params=pltpu.CompilerParams(vmem_limit_bytes=32 * 1024 * 1024),
        cost_estimate=small_cost(),
    )(totals, *taken)


def local(
    n_el,
    n_ph,
    elec_dev,
    phon_dev,
    elec_source,
    phon_source,
    elec_rate,
    phon_rate,
    tiles,
    tile_rows,
    tile_cols,
    tile_count,
):
    tile_set = tiles[0, 0]
    slots = tile_set.shape[0]
    group = math.gcd(slots, 16)
    elec_span = elec_dev.shape[0]
    phon_span = phon_dev.shape[1]
    elec_blocks = elec_span * n_ph
    phon_blocks = phon_span * n_el
    cores = 2 if n_ph % 2 == 0 else 1
    n_z = n_ph // cores
    el_place = lax.axis_index("el")
    ph_place = lax.axis_index("ph")
    z_place, core_place = ph_place // cores, ph_place % cores

    live = jnp.arange(slots, dtype=jnp.int32) < tile_count[0, 0]
    row_ids, col_ids = tile_rows[0, 0], tile_cols[0, 0]
    col_owner = col_ids // phon_span
    row_owner = row_ids // elec_span
    row_z, row_core = row_owner // cores, row_owner % cores
    if n_el & (n_el - 1) == 0:
        phon_in = phon_out = col_owner ^ el_place
    else:
        phon_in, phon_out = (el_place - col_owner) % n_el, (col_owner - el_place) % n_el
    if n_z & (n_z - 1) == 0:
        elec_in = elec_out = row_z ^ z_place
    else:
        elec_in, elec_out = (z_place - row_z) % n_z, (row_z - z_place) % n_z
    other_core = (row_core != core_place).astype(jnp.int32)
    phon_in = phon_in * phon_span + col_ids % phon_span
    phon_out = phon_out * phon_span + col_ids % phon_span
    elec_in = (other_core * n_z + elec_in) * elec_span + row_ids % elec_span
    elec_out = (other_core * n_z + elec_out) * elec_span + row_ids % elec_span
    phon_out = jnp.where(live, phon_out, phon_blocks)
    elec_out = jnp.where(live, elec_out, elec_blocks)
    group_count = (tile_count[0] + (group - 1)) // group

    def after(values, first):
        return list(lax.optimization_barrier((list(values), list(first)))[0])

    def over_el(values):
        return [
            send(value, "el", n_el, partner(n_el, step + 1)) for step, value in enumerate(values)
        ]

    def over_z(values):
        def place_of(step):
            z_of = partner(n_z, step)
            return lambda place: z_of(place // cores) * cores + place % cores

        return [send(value, "ph", n_ph, place_of(step + 1)) for step, value in enumerate(values)]

    def over_core(value):
        return send(value, "ph", n_ph, lambda place: place ^ 1)

    def spread_phon(value):
        half = phon_span // 2
        if RELAY and n_el == 4 and half:
            near, far = over_el([value] * 2)
            halves = after([far[:half], near[half:]], [near, far])
            passed = [
                send(piece, "el", n_el, partner(n_el, step + 1)) for step, piece in enumerate(halves)
            ]
            return [value, near, far, *passed], halves
        pieces = [value] + over_el([value] * (n_el - 1))
        return pieces, pieces[1:2]

    def spread_elec(value, first):
        same_core = [value] + over_z([value] * (n_z - 1))
        if cores == 1:
            return same_core
        others = after(same_core[1:], first)
        return same_core + [over_core(piece) for piece in [value] + others]

    elec_terms = [[(step, index) for step in range(n_z - 1)] for index in range(elec_span)]
    half = phon_span // 2
    relay = RELAY and n_el == 4 and phon_span % 2 == 0
    near, far, both = phon_span, 2 * phon_span, 3 * phon_span
    if relay:
        plan = [
            [start + index for start in (both, near) for index in range(half)],
            [start + index for start in (both, far) for index in range(half, phon_span)],
        ]
        combined = [list(range(half)), list(range(half, phon_span))]
        phon_terms = [[(0, half + index), (3, index)] for index in range(half)]
        phon_terms += [[(1, half + index), (2, index)] for index in range(half)]
    else:
        plan = [
            list(range((step + 1) * phon_span, (step + 2) * phon_span)) for step in range(n_el - 1)
        ]
        phon_terms = [[(step, index) for step in range(n_el - 1)] for index in range(phon_span)]
    middle = elec_blocks // 2
    kept = (
        [(0, middle), (middle, elec_blocks)],
        [(0, phon_span)] + [(near + half, far + half)] * relay,
        plan,
    )
    ids = (elec_in, elec_out, phon_in, phon_out, group_count)
    elec_now, phon_now = elec_dev.astype(jnp.bfloat16), phon_dev[0].astype(jnp.bfloat16)
    for sweep in range(ITERS):
        dtype = jnp.bfloat16 if sweep + 1 < ITERS else jnp.float32
        phon_pieces, passed = spread_phon(phon_now)
        elec_pieces = spread_elec(elec_now, passed)
        (elec_own, given), phon_own, phon_coded = drags(
            ids, tile_set, group, elec_pieces, phon_pieces, kept
        )
        theirs = over_core(given)
        elec_own, *elec_coded = pair_sum(elec_own, theirs, n_z - 1)
        elec_coded = over_z(elec_coded)
        phon_coded = over_el(phon_coded)
        if relay:
            taken = after(phon_coded[::-1], [elec_own, *elec_coded[:EARLY]])
            phon_coded += over_el(combine(phon_own[1], taken, combined))
        (phon_kept,) = after(phon_own[:1], [elec_own, *elec_coded[:TIES]])
        phon_now = renew(phon_source[0], phon_kept, phon_coded, phon_terms, phon_rate[0], dtype)
        (elec_own,) = after([elec_own], [phon_now])
        elec_now = renew(elec_source, elec_own, elec_coded, elec_terms, elec_rate, dtype)
    return (elec_now, phon_now[None])


def solution(mesh):
    in_specs = (
        P(("el", "ph"), None, None),
        P("ph", "el", None, None),
        P(("el", "ph"), None, None),
        P("ph", "el", None, None),
        P(("el", "ph"), None),
        P("ph", "el", None),
        P("el", "ph", None, None, None),
        P("el", "ph", None),
        P("el", "ph", None),
        P("el", "ph"),
    )
    out_specs = (P(("el", "ph"), None, None), P("ph", "el", None, None))
    body = functools.partial(local, mesh.shape["el"], mesh.shape["ph"])
    return jax.shard_map(body, mesh=mesh, in_specs=in_specs, out_specs=out_specs, check_vma=False)
```

```python
import functools
import math

import jax
import jax.numpy as jnp
from jax import lax
from jax.experimental import pallas as pl
from jax.experimental.pallas import tpu as pltpu
from jax.sharding import PartitionSpec as P

ITERS = 3
DEPTH = 3
COST = 1024
LEVELS = 32000.0
HIGHEST = 126.0
TAIL = 16
TIES = 3
EARLY = 2
RELAY = True
SMALLEST = 1e-33


def partner(size, step):
    if size & (size - 1) == 0:
        return lambda place: place ^ step
    return lambda place: (place + step) % size


def send(value, axis, size, place_of):
    return lax.ppermute(value, axis, [(place, place_of(place)) for place in range(size)])


def encode_piece(block_of, size, coded):
    rows, lanes = block_of(0).shape
    row = lax.broadcasted_iota(jnp.int32, (TAIL, lanes), 0)
    tails = [jnp.zeros((TAIL, lanes), jnp.float32) for _ in range(tail_rows(size) // TAIL)]
    for index in range(size):
        block = block_of(index)
        peak = jnp.maximum(jnp.max(jnp.abs(block), axis=0, keepdims=True), SMALLEST)
        power = jnp.minimum(jnp.floor(jnp.log2(peak)) + 1.0, HIGHEST)
        scaled = jnp.round(block * (jnp.exp2(-power) * LEVELS))
        coded[pl.ds(index * rows, rows), :] = scaled.astype(jnp.int32).astype(jnp.int16)
        tails[index // TAIL] = jnp.where(row == index % TAIL, power, tails[index // TAIL])
    for index, tail in enumerate(tails):
        coded[pl.ds(size * rows + index * TAIL, TAIL), :] = tail.astype(jnp.int32).astype(jnp.int16)


def scales_of(coded, size, rows):
    tails = [
        coded[pl.ds(size * rows + index * TAIL, TAIL), :].astype(jnp.int32).astype(jnp.float32)
        for index in range(tail_rows(size) // TAIL)
    ]
    return [
        jnp.exp2(tails[index // TAIL][index % TAIL : index % TAIL + 1]) * (1.0 / LEVELS)
        for index in range(size)
    ]


def tail_rows(size):
    return -(-size // TAIL) * TAIL


def drags_body(group, counts, kept, *refs):
    elec_pieces, phon_pieces = counts
    elec_kept, phon_kept, plan = kept
    elec_in, elec_out, phon_in, phon_out, group_count, tiles = refs[:6]
    refs = refs[6:]
    sources, refs = refs[: elec_pieces + phon_pieces], refs[elec_pieces + phon_pieces :]
    whole, refs = refs[: len(elec_kept) + len(phon_kept)], refs[len(elec_kept) + len(phon_kept) :]
    coded, refs = refs[: len(plan)], refs[len(plan) :]
    elec, phon, elec_totals, phon_totals, held, tile_sems, out_sems = refs
    groups = group_count[0]

    def fetch(index):
        slot = lax.rem(index, DEPTH)
        return pltpu.make_async_copy(
            tiles.at[pl.ds(index * group, group)], held.at[slot], tile_sems.at[slot]
        )

    for ahead in range(DEPTH - 1):

        @pl.when(ahead < groups)
        def _():
            fetch(ahead).start()

    for target, pieces in ((elec, sources[:elec_pieces]), (phon, sources[elec_pieces:])):
        first = 0
        for piece in pieces:
            span = piece.shape[0]
            target[pl.ds(first, span)] = piece[...]
            first += span
    elec_totals[...] = jnp.zeros_like(elec_totals)
    phon_totals[...] = jnp.zeros_like(phon_totals)

    def one_group(index, carry):
        @pl.when(index + DEPTH - 1 < groups)
        def _():
            fetch(index + DEPTH - 1).start()

        fetch(index).wait()
        slot = lax.rem(index, DEPTH)
        for inner in range(group):
            place = index * group + inner
            tile = held[slot, inner]
            to_phon = lax.dot_general(
                elec[elec_in[place]], tile, (((1,), (0,)), ((), ())),
                preferred_element_type=jnp.float32,
            )
            to_elec = lax.dot_general(
                phon[phon_in[place]], tile, (((1,), (1,)), ((), ())),
                preferred_element_type=jnp.float32,
            )
            target = phon_out[place]
            phon_totals[target] = phon_totals[target] + to_phon
            target = elec_out[place]
            elec_totals[target] = elec_totals[target] + to_elec
        return carry

    lax.fori_loop(0, groups, one_group, 0)
    places = [(elec_totals, span) for span in elec_kept] + [(phon_totals, span) for span in phon_kept]
    stores = [
        pltpu.make_async_copy(
            totals.at[pl.ds(first, end - first)], whole[index], out_sems.at[index]
        )
        for index, (totals, (first, end)) in enumerate(places)
    ]
    for store in stores:
        store.start()
    for blocks, piece in zip(plan, coded):
        encode_piece(lambda index, blocks=blocks: phon_totals[blocks[index]], len(blocks), piece)
    for store in stores:
        store.wait()


def drags(ids, tile_set, group, elec_pieces, phon_pieces, kept):
    elec_kept, phon_kept, plan = kept
    _, rows, lanes = elec_pieces[0].shape
    side = tile_set.shape[-1]
    elec_blocks = sum(piece.shape[0] for piece in elec_pieces)
    phon_blocks = sum(piece.shape[0] for piece in phon_pieces)
    any_space = pl.BlockSpec(memory_space=pl.ANY)
    smem = pl.BlockSpec(memory_space=pltpu.SMEM)
    vmem = pl.BlockSpec(memory_space=pltpu.VMEM)
    pieces = list(elec_pieces) + list(phon_pieces)
    whole = list(elec_kept) + list(phon_kept)
    outs = pl.pallas_call(
        functools.partial(drags_body, group, (len(elec_pieces), len(phon_pieces)), kept),
        out_shape=[
            jax.ShapeDtypeStruct((end - first, rows, lanes), jnp.float32) for first, end in whole
        ]
        + [coded_shape(len(blocks), rows, lanes) for blocks in plan],
        in_specs=[smem] * 5 + [any_space] + [vmem] * len(pieces),
        out_specs=[any_space] * len(whole) + [vmem] * len(plan),
        scratch_shapes=[
            pltpu.VMEM((elec_blocks, rows, lanes), jnp.bfloat16),
            pltpu.VMEM((phon_blocks, rows, lanes), jnp.bfloat16),
            pltpu.VMEM((elec_blocks + 1, rows, lanes), jnp.float32),
            pltpu.VMEM((phon_blocks + 1, rows, lanes), jnp.float32),
            pltpu.VMEM((DEPTH, group, side, side), jnp.bfloat16),
            pltpu.SemaphoreType.DMA((DEPTH,)),
            pltpu.SemaphoreType.DMA((len(whole),)),
        ],
        compiler_params=pltpu.CompilerParams(vmem_limit_bytes=40 * 1024 * 1024),
        cost_estimate=pl.CostEstimate(
            flops=4 * tile_set.shape[0] * rows * side * side,
            bytes_accessed=2 * tile_set.shape[0] * side * side * 2,
            transcendentals=0,
        ),
    )(*ids, tile_set, *pieces)
    return outs[: len(elec_kept)], outs[len(elec_kept) : len(whole)], outs[len(whole) :]


def coded_shape(size, rows, lanes):
    return jax.ShapeDtypeStruct((size * rows + tail_rows(size), lanes), jnp.int16)


def drag(ids_in, ids_out, group_count, tile_set, group, pieces, transposed, whole_sizes, coded_sizes):
    _, rows, lanes = pieces[0].shape
    blocks_in = sum(piece.shape[0] for piece in pieces)
    blocks_out = sum(whole_sizes) + sum(coded_sizes)
    any_space = pl.BlockSpec(memory_space=pl.ANY)
    smem = pl.BlockSpec(memory_space=pltpu.SMEM)
    vmem = pl.BlockSpec(memory_space=pltpu.VMEM)
    side = tile_set.shape[-1]
    return pl.pallas_call(
        functools.partial(
            drag_body, len(pieces), group, transposed, len(whole_sizes), coded_sizes
        ),
        out_shape=[jax.ShapeDtypeStruct((size, rows, lanes), jnp.float32) for size in whole_sizes]
        + [coded_shape(size, rows, lanes) for size in coded_sizes],
        in_specs=[smem, smem, smem, any_space] + [any_space] * len(pieces),
        out_specs=[any_space] * len(whole_sizes) + [vmem] * len(coded_sizes),
        scratch_shapes=[
            pltpu.VMEM((blocks_in, rows, lanes), jnp.bfloat16),
            pltpu.VMEM((blocks_out + 1, rows, lanes), jnp.float32),
            pltpu.VMEM((DEPTH, group, side, side), jnp.bfloat16),
            pltpu.SemaphoreType.DMA((DEPTH,)),
            pltpu.SemaphoreType.DMA((max(len(whole_sizes), 1),)),
        ],
        compiler_params=pltpu.CompilerParams(vmem_limit_bytes=40 * 1024 * 1024),
        cost_estimate=pl.CostEstimate(
            flops=2 * tile_set.shape[0] * rows * side * side,
            bytes_accessed=2 * tile_set.shape[0] * side * side * 2,
            transcendentals=0,
        ),
    )(ids_in, ids_out, group_count, tile_set, *pieces)


def pair_body(mine, theirs, whole, *coded):
    span = whole.shape[0]
    whole[...] = mine[pl.ds(0, span)] + theirs[pl.ds(0, span)]
    for index, piece in enumerate(coded):
        first = (index + 1) * span
        encode_piece(lambda block, first=first: mine[first + block] + theirs[first + block], span, piece)


def pair_sum(mine, theirs, piece_count):
    blocks, rows, lanes = theirs.shape
    span = blocks // (piece_count + 1)
    vmem = pl.BlockSpec(memory_space=pltpu.VMEM)
    return pl.pallas_call(
        pair_body,
        out_shape=[jax.ShapeDtypeStruct((span, rows, lanes), jnp.float32)]
        + [coded_shape(span, rows, lanes)] * piece_count,
        in_specs=[vmem, vmem],
        out_specs=[vmem] * (1 + piece_count),
        compiler_params=pltpu.CompilerParams(vmem_limit_bytes=32 * 1024 * 1024),
        cost_estimate=small_cost(),
    )(mine, theirs)


def small_cost():
    return pl.CostEstimate(flops=COST, bytes_accessed=COST, transcendentals=0)


def decode(piece, index, scales, rows):
    values = piece[pl.ds(index * rows, rows), :].astype(jnp.int32).astype(jnp.float32)
    return values * scales[index]


def piece_size(piece, rows):
    return next(size for size in range(piece.shape[0] // rows + 1) if size * rows + tail_rows(size) == piece.shape[0])


def renew_body(terms, source, own, rate, *refs):
    coded, result = refs[:-1], refs[-1]
    _, rows, _ = result.shape
    scales = [scales_of(piece, piece_size(piece, rows), rows) for piece in coded]
    for index, parts in enumerate(terms):
        total = own[index]
        for piece, place in parts:
            total = total + decode(coded[piece], place, scales[piece], rows)
        fresh = (source[index] + total) / rate[pl.ds(index, 1), :]
        result[index] = fresh.astype(result.dtype)


def renew(source, own, coded, terms, rate, dtype):
    vmem = pl.BlockSpec(memory_space=pltpu.VMEM)
    return pl.pallas_call(
        functools.partial(renew_body, terms),
        out_shape=jax.ShapeDtypeStruct(source.shape, dtype),
        in_specs=[vmem] * (3 + len(coded)),
        out_specs=vmem,
        compiler_params=pltpu.CompilerParams(vmem_limit_bytes=32 * 1024 * 1024),
        cost_estimate=small_cost(),
    )(source, own, rate, *coded)


def combine_body(plan, totals, *refs):
    taken, given = refs[: len(plan)], refs[len(plan) :]
    _, rows, _ = totals.shape
    for blocks, source, target in zip(plan, taken, given):
        scales = scales_of(source, piece_size(source, rows), rows)
        encode_piece(
            lambda index, blocks=blocks, source=source, scales=scales: totals[blocks[index]]
            + decode(source, index, scales, rows),
            len(blocks), target,
        )


def combine(totals, taken, plan):
    _, rows, lanes = totals.shape
    vmem = pl.BlockSpec(memory_space=pltpu.VMEM)
    return pl.pallas_call(
        functools.partial(combine_body, plan),
        out_shape=[coded_shape(len(blocks), rows, lanes) for blocks in plan],
        in_specs=[vmem] * (1 + len(taken)),
        out_specs=[vmem] * len(plan),
        compiler_params=pltpu.CompilerParams(vmem_limit_bytes=32 * 1024 * 1024),
        cost_estimate=small_cost(),
    )(totals, *taken)


def split_body(near, far, first, second):
    half = first.shape[0]
    first[...] = far[pl.ds(0, half)]
    second[...] = near[pl.ds(half, second.shape[0])]


def split(near, far, half):
    blocks, rows, lanes = near.shape
    vmem = pl.BlockSpec(memory_space=pltpu.VMEM)
    return pl.pallas_call(
        split_body,
        out_shape=[
            jax.ShapeDtypeStruct((size, rows, lanes), near.dtype) for size in (half, blocks - half)
        ],
        in_specs=[vmem] * 2,
        out_specs=[vmem] * 2,
        compiler_params=pltpu.CompilerParams(vmem_limit_bytes=32 * 1024 * 1024),
        cost_estimate=small_cost(),
    )(near, far)


def local(
    n_el,
    n_ph,
    elec_dev,
    phon_dev,
    elec_source,
    phon_source,
    elec_rate,
    phon_rate,
    tiles,
    tile_rows,
    tile_cols,
    tile_count,
):
    tile_set = tiles[0, 0]
    slots = tile_set.shape[0]
    group = math.gcd(slots, 16)
    elec_span = elec_dev.shape[0]
    phon_span = phon_dev.shape[1]
    elec_blocks = elec_span * n_ph
    phon_blocks = phon_span * n_el
    cores = 2 if n_ph % 2 == 0 else 1
    n_z = n_ph // cores
    el_place = lax.axis_index("el")
    ph_place = lax.axis_index("ph")
    z_place, core_place = ph_place // cores, ph_place % cores

    live = jnp.arange(slots, dtype=jnp.int32) < tile_count[0, 0]
    row_ids, col_ids = tile_rows[0, 0], tile_cols[0, 0]
    col_owner = col_ids // phon_span
    row_owner = row_ids // elec_span
    row_z, row_core = row_owner // cores, row_owner % cores
    if n_el & (n_el - 1) == 0:
        phon_in = phon_out = col_owner ^ el_place
    else:
        phon_in, phon_out = (el_place - col_owner) % n_el, (col_owner - el_place) % n_el
    if n_z & (n_z - 1) == 0:
        elec_in = elec_out = row_z ^ z_place
    else:
        elec_in, elec_out = (z_place - row_z) % n_z, (row_z - z_place) % n_z
    other_core = (row_core != core_place).astype(jnp.int32)
    phon_in = phon_in * phon_span + col_ids % phon_span
    phon_out = phon_out * phon_span + col_ids % phon_span
    elec_in = (other_core * n_z + elec_in) * elec_span + row_ids % elec_span
    elec_out = (other_core * n_z + elec_out) * elec_span + row_ids % elec_span
    phon_out = jnp.where(live, phon_out, phon_blocks)
    elec_out = jnp.where(live, elec_out, elec_blocks)
    group_count = (tile_count[0] + (group - 1)) // group

    def after(values, first):
        return list(lax.optimization_barrier((list(values), list(first)))[0])

    def over_el(values):
        return [
            send(value, "el", n_el, partner(n_el, step + 1)) for step, value in enumerate(values)
        ]

    def over_z(values):
        def place_of(step):
            z_of = partner(n_z, step)
            return lambda place: z_of(place // cores) * cores + place % cores

        return [send(value, "ph", n_ph, place_of(step + 1)) for step, value in enumerate(values)]

    def over_core(value):
        return send(value, "ph", n_ph, lambda place: place ^ 1)

    def spread_phon(value):
        half = phon_span // 2
        if RELAY and n_el == 4 and half:
            near, far = over_el([value] * 2)
            halves = split(near, far, half)
            passed = [
                send(piece, "el", n_el, partner(n_el, step + 1)) for step, piece in enumerate(halves)
            ]
            return [value, near, far, *passed], halves
        pieces = [value] + over_el([value] * (n_el - 1))
        return pieces, pieces[1:2]

    def spread_elec(value, first):
        same_core = [value] + over_z([value] * (n_z - 1))
        if cores == 1:
            return same_core
        others = after(same_core[1:], first)
        return same_core + [over_core(piece) for piece in [value] + others]

    elec_terms = [[(step, index) for step in range(n_z - 1)] for index in range(elec_span)]
    half = phon_span // 2
    relay = RELAY and n_el == 4 and phon_span % 2 == 0
    near, far, both = phon_span, 2 * phon_span, 3 * phon_span
    if relay:
        plan = [
            [start + index for start in (both, near) for index in range(half)],
            [start + index for start in (both, far) for index in range(half, phon_span)],
        ]
        combined = [list(range(half)), list(range(half, phon_span))]
        phon_terms = [[(0, half + index), (3, index)] for index in range(half)]
        phon_terms += [[(1, half + index), (2, index)] for index in range(half)]
    else:
        plan = [
            list(range((step + 1) * phon_span, (step + 2) * phon_span)) for step in range(n_el - 1)
        ]
        phon_terms = [[(step, index) for step in range(n_el - 1)] for index in range(phon_span)]
    middle = elec_blocks // 2
    kept = (
        [(0, middle), (middle, elec_blocks)],
        [(0, phon_span)] + [(near + half, far + half)] * relay,
        plan,
    )
    ids = (elec_in, elec_out, phon_in, phon_out, group_count)
    elec_now, phon_now = elec_dev.astype(jnp.bfloat16), phon_dev[0].astype(jnp.bfloat16)
    for sweep in range(ITERS):
        dtype = jnp.bfloat16 if sweep + 1 < ITERS else jnp.float32
        phon_pieces, passed = spread_phon(phon_now)
        elec_pieces = spread_elec(elec_now, passed)
        (elec_own, given), phon_own, phon_coded = drags(
            ids, tile_set, group, elec_pieces, phon_pieces, kept
        )
        theirs = over_core(given)
        elec_own, *elec_coded = pair_sum(elec_own, theirs, n_z - 1)
        elec_coded = over_z(elec_coded)
        phon_coded = over_el(phon_coded)
        if relay:
            taken = after(phon_coded[::-1], [elec_own, *elec_coded[:EARLY]])
            phon_coded += over_el(combine(phon_own[1], taken, combined))
        (phon_kept,) = after(phon_own[:1], [elec_own, *elec_coded[:TIES]])
        phon_now = renew(phon_source[0], phon_kept, phon_coded, phon_terms, phon_rate[0], dtype)
        (elec_own,) = after([elec_own], [phon_now])
        elec_now = renew(elec_source, elec_own, elec_coded, elec_terms, elec_rate, dtype)
    return (elec_now, phon_now[None])


def solution(mesh):
    in_specs = (
        P(("el", "ph"), None, None),
        P("ph", "el", None, None),
        P(("el", "ph"), None, None),
        P("ph", "el", None, None),
        P(("el", "ph"), None),
        P("ph", "el", None),
        P("el", "ph", None, None, None),
        P("el", "ph", None),
        P("el", "ph", None),
        P("el", "ph"),
    )
    out_specs = (P(("el", "ph"), None, None), P("ph", "el", None, None))
    body = functools.partial(local, mesh.shape["el"], mesh.shape["ph"])
    return jax.shard_map(body, mesh=mesh, in_specs=in_specs, out_specs=out_specs, check_vma=False)
```

```python
import functools
import math

import jax
import jax.numpy as jnp
from jax import lax
from jax.experimental import pallas as pl
from jax.experimental.pallas import tpu as pltpu
from jax.sharding import PartitionSpec as P

ITERS = 3
DEPTH = 3
COST = 1024
LEVELS = 32000.0
HIGHEST = 126.0
TAIL = 16
TIES = 3
EARLY = 2
RELAY = True
SMALLEST = 1e-33


def partner(size, step):
    if size & (size - 1) == 0:
        return lambda place: place ^ step
    return lambda place: (place + step) % size


def send(value, axis, size, place_of):
    return lax.ppermute(value, axis, [(place, place_of(place)) for place in range(size)])


def encode_piece(block_of, size, coded):
    rows, lanes = block_of(0).shape
    row = lax.broadcasted_iota(jnp.int32, (TAIL, lanes), 0)
    tails = [jnp.zeros((TAIL, lanes), jnp.float32) for _ in range(tail_rows(size) // TAIL)]
    for index in range(size):
        block = block_of(index)
        peak = jnp.maximum(jnp.max(jnp.abs(block), axis=0, keepdims=True), SMALLEST)
        power = jnp.minimum(jnp.floor(jnp.log2(peak)) + 1.0, HIGHEST)
        scaled = jnp.round(block * (jnp.exp2(-power) * LEVELS))
        coded[pl.ds(index * rows, rows), :] = scaled.astype(jnp.int32).astype(jnp.int16)
        tails[index // TAIL] = jnp.where(row == index % TAIL, power, tails[index // TAIL])
    for index, tail in enumerate(tails):
        coded[pl.ds(size * rows + index * TAIL, TAIL), :] = tail.astype(jnp.int32).astype(jnp.int16)


def scales_of(coded, size, rows):
    tails = [
        coded[pl.ds(size * rows + index * TAIL, TAIL), :].astype(jnp.int32).astype(jnp.float32)
        for index in range(tail_rows(size) // TAIL)
    ]
    return [
        jnp.exp2(tails[index // TAIL][index % TAIL : index % TAIL + 1]) * (1.0 / LEVELS)
        for index in range(size)
    ]


def tail_rows(size):
    return -(-size // TAIL) * TAIL


def drags_body(group, counts, kept, *refs):
    elec_pieces, phon_pieces = counts
    elec_kept, phon_kept, plan = kept
    elec_in, elec_out, phon_in, phon_out, group_count, tiles = refs[:6]
    refs = refs[6:]
    sources, refs = refs[: elec_pieces + phon_pieces], refs[elec_pieces + phon_pieces :]
    whole, refs = refs[: len(elec_kept) + len(phon_kept)], refs[len(elec_kept) + len(phon_kept) :]
    coded, refs = refs[: len(plan)], refs[len(plan) :]
    elec, phon, elec_totals, phon_totals, held, tile_sems = refs
    groups = group_count[0]

    def fetch(index):
        slot = lax.rem(index, DEPTH)
        return pltpu.make_async_copy(
            tiles.at[pl.ds(index * group, group)], held.at[slot], tile_sems.at[slot]
        )

    for ahead in range(DEPTH - 1):

        @pl.when(ahead < groups)
        def _():
            fetch(ahead).start()

    for target, pieces in ((elec, sources[:elec_pieces]), (phon, sources[elec_pieces:])):
        first = 0
        for piece in pieces:
            span = piece.shape[0]
            target[pl.ds(first, span)] = piece[...]
            first += span
    elec_totals[...] = jnp.zeros_like(elec_totals)
    phon_totals[...] = jnp.zeros_like(phon_totals)

    def one_group(index, carry):
        @pl.when(index + DEPTH - 1 < groups)
        def _():
            fetch(index + DEPTH - 1).start()

        fetch(index).wait()
        slot = lax.rem(index, DEPTH)
        for inner in range(group):
            place = index * group + inner
            tile = held[slot, inner]
            to_phon = lax.dot_general(
                elec[elec_in[place]], tile, (((1,), (0,)), ((), ())),
                preferred_element_type=jnp.float32,
            )
            to_elec = lax.dot_general(
                phon[phon_in[place]], tile, (((1,), (1,)), ((), ())),
                preferred_element_type=jnp.float32,
            )
            target = phon_out[place]
            phon_totals[target] = phon_totals[target] + to_phon
            target = elec_out[place]
            elec_totals[target] = elec_totals[target] + to_elec
        return carry

    lax.fori_loop(0, groups, one_group, 0)
    places = [(elec_totals, span) for span in elec_kept] + [(phon_totals, span) for span in phon_kept]
    for target, (totals, (first, end)) in zip(whole, places):
        target[...] = totals[pl.ds(first, end - first)]
    for blocks, piece in zip(plan, coded):
        encode_piece(lambda index, blocks=blocks: phon_totals[blocks[index]], len(blocks), piece)


def drags(ids, tile_set, group, elec_pieces, phon_pieces, kept):
    elec_kept, phon_kept, plan = kept
    _, rows, lanes = elec_pieces[0].shape
    side = tile_set.shape[-1]
    elec_blocks = sum(piece.shape[0] for piece in elec_pieces)
    phon_blocks = sum(piece.shape[0] for piece in phon_pieces)
    any_space = pl.BlockSpec(memory_space=pl.ANY)
    smem = pl.BlockSpec(memory_space=pltpu.SMEM)
    vmem = pl.BlockSpec(memory_space=pltpu.VMEM)
    pieces = list(elec_pieces) + list(phon_pieces)
    whole = list(elec_kept) + list(phon_kept)
    outs = pl.pallas_call(
        functools.partial(drags_body, group, (len(elec_pieces), len(phon_pieces)), kept),
        out_shape=[
            jax.ShapeDtypeStruct((end - first, rows, lanes), jnp.float32) for first, end in whole
        ]
        + [coded_shape(len(blocks), rows, lanes) for blocks in plan],
        in_specs=[smem] * 5 + [any_space] + [vmem] * len(pieces),
        out_specs=[vmem] * (len(whole) + len(plan)),
        scratch_shapes=[
            pltpu.VMEM((elec_blocks, rows, lanes), jnp.bfloat16),
            pltpu.VMEM((phon_blocks, rows, lanes), jnp.bfloat16),
            pltpu.VMEM((elec_blocks + 1, rows, lanes), jnp.float32),
            pltpu.VMEM((phon_blocks + 1, rows, lanes), jnp.float32),
            pltpu.VMEM((DEPTH, group, side, side), jnp.bfloat16),
            pltpu.SemaphoreType.DMA((DEPTH,)),
        ],
        compiler_params=pltpu.CompilerParams(vmem_limit_bytes=40 * 1024 * 1024),
        cost_estimate=pl.CostEstimate(
            flops=4 * tile_set.shape[0] * rows * side * side,
            bytes_accessed=2 * tile_set.shape[0] * side * side * 2,
            transcendentals=0,
        ),
    )(*ids, tile_set, *pieces)
    return outs[: len(elec_kept)], outs[len(elec_kept) : len(whole)], outs[len(whole) :]


def coded_shape(size, rows, lanes):
    return jax.ShapeDtypeStruct((size * rows + tail_rows(size), lanes), jnp.int16)


def drag(ids_in, ids_out, group_count, tile_set, group, pieces, transposed, whole_sizes, coded_sizes):
    _, rows, lanes = pieces[0].shape
    blocks_in = sum(piece.shape[0] for piece in pieces)
    blocks_out = sum(whole_sizes) + sum(coded_sizes)
    any_space = pl.BlockSpec(memory_space=pl.ANY)
    smem = pl.BlockSpec(memory_space=pltpu.SMEM)
    vmem = pl.BlockSpec(memory_space=pltpu.VMEM)
    side = tile_set.shape[-1]
    return pl.pallas_call(
        functools.partial(
            drag_body, len(pieces), group, transposed, len(whole_sizes), coded_sizes
        ),
        out_shape=[jax.ShapeDtypeStruct((size, rows, lanes), jnp.float32) for size in whole_sizes]
        + [coded_shape(size, rows, lanes) for size in coded_sizes],
        in_specs=[smem, smem, smem, any_space] + [any_space] * len(pieces),
        out_specs=[any_space] * len(whole_sizes) + [vmem] * len(coded_sizes),
        scratch_shapes=[
            pltpu.VMEM((blocks_in, rows, lanes), jnp.bfloat16),
            pltpu.VMEM((blocks_out + 1, rows, lanes), jnp.float32),
            pltpu.VMEM((DEPTH, group, side, side), jnp.bfloat16),
            pltpu.SemaphoreType.DMA((DEPTH,)),
            pltpu.SemaphoreType.DMA((max(len(whole_sizes), 1),)),
        ],
        compiler_params=pltpu.CompilerParams(vmem_limit_bytes=40 * 1024 * 1024),
        cost_estimate=pl.CostEstimate(
            flops=2 * tile_set.shape[0] * rows * side * side,
            bytes_accessed=2 * tile_set.shape[0] * side * side * 2,
            transcendentals=0,
        ),
    )(ids_in, ids_out, group_count, tile_set, *pieces)


def pair_body(mine, theirs, whole, *coded):
    span = whole.shape[0]
    whole[...] = mine[pl.ds(0, span)] + theirs[pl.ds(0, span)]
    for index, piece in enumerate(coded):
        first = (index + 1) * span
        encode_piece(lambda block, first=first: mine[first + block] + theirs[first + block], span, piece)


def pair_sum(mine, theirs, piece_count):
    blocks, rows, lanes = theirs.shape
    span = blocks // (piece_count + 1)
    vmem = pl.BlockSpec(memory_space=pltpu.VMEM)
    return pl.pallas_call(
        pair_body,
        out_shape=[jax.ShapeDtypeStruct((span, rows, lanes), jnp.float32)]
        + [coded_shape(span, rows, lanes)] * piece_count,
        in_specs=[vmem, vmem],
        out_specs=[vmem] * (1 + piece_count),
        compiler_params=pltpu.CompilerParams(vmem_limit_bytes=32 * 1024 * 1024),
        cost_estimate=small_cost(),
    )(mine, theirs)


def small_cost():
    return pl.CostEstimate(flops=COST, bytes_accessed=COST, transcendentals=0)


def decode(piece, index, scales, rows):
    values = piece[pl.ds(index * rows, rows), :].astype(jnp.int32).astype(jnp.float32)
    return values * scales[index]


def piece_size(piece, rows):
    return next(size for size in range(piece.shape[0] // rows + 1) if size * rows + tail_rows(size) == piece.shape[0])


def renew_body(terms, source, own, rate, *refs):
    coded, result = refs[:-1], refs[-1]
    _, rows, _ = result.shape
    scales = [scales_of(piece, piece_size(piece, rows), rows) for piece in coded]
    for index, parts in enumerate(terms):
        total = own[index]
        for piece, place in parts:
            total = total + decode(coded[piece], place, scales[piece], rows)
        fresh = (source[index] + total) / rate[pl.ds(index, 1), :]
        result[index] = fresh.astype(result.dtype)


def renew(source, own, coded, terms, rate, dtype):
    vmem = pl.BlockSpec(memory_space=pltpu.VMEM)
    return pl.pallas_call(
        functools.partial(renew_body, terms),
        out_shape=jax.ShapeDtypeStruct(source.shape, dtype),
        in_specs=[vmem] * (3 + len(coded)),
        out_specs=vmem,
        compiler_params=pltpu.CompilerParams(vmem_limit_bytes=32 * 1024 * 1024),
        cost_estimate=small_cost(),
    )(source, own, rate, *coded)


def combine_body(plan, totals, *refs):
    taken, given = refs[: len(plan)], refs[len(plan) :]
    _, rows, _ = totals.shape
    for blocks, source, target in zip(plan, taken, given):
        scales = scales_of(source, piece_size(source, rows), rows)
        encode_piece(
            lambda index, blocks=blocks, source=source, scales=scales: totals[blocks[index]]
            + decode(source, index, scales, rows),
            len(blocks), target,
        )


def combine(totals, taken, plan):
    _, rows, lanes = totals.shape
    vmem = pl.BlockSpec(memory_space=pltpu.VMEM)
    return pl.pallas_call(
        functools.partial(combine_body, plan),
        out_shape=[coded_shape(len(blocks), rows, lanes) for blocks in plan],
        in_specs=[vmem] * (1 + len(taken)),
        out_specs=[vmem] * len(plan),
        compiler_params=pltpu.CompilerParams(vmem_limit_bytes=32 * 1024 * 1024),
        cost_estimate=small_cost(),
    )(totals, *taken)


def split_body(near, far, first, second):
    half = first.shape[0]
    first[...] = far[pl.ds(0, half)]
    second[...] = near[pl.ds(half, second.shape[0])]


def split(near, far, half):
    blocks, rows, lanes = near.shape
    vmem = pl.BlockSpec(memory_space=pltpu.VMEM)
    return pl.pallas_call(
        split_body,
        out_shape=[
            jax.ShapeDtypeStruct((size, rows, lanes), near.dtype) for size in (half, blocks - half)
        ],
        in_specs=[vmem] * 2,
        out_specs=[vmem] * 2,
        compiler_params=pltpu.CompilerParams(vmem_limit_bytes=32 * 1024 * 1024),
        cost_estimate=small_cost(),
    )(near, far)


def local(
    n_el,
    n_ph,
    elec_dev,
    phon_dev,
    elec_source,
    phon_source,
    elec_rate,
    phon_rate,
    tiles,
    tile_rows,
    tile_cols,
    tile_count,
):
    tile_set = tiles[0, 0]
    slots = tile_set.shape[0]
    group = math.gcd(slots, 16)
    elec_span = elec_dev.shape[0]
    phon_span = phon_dev.shape[1]
    elec_blocks = elec_span * n_ph
    phon_blocks = phon_span * n_el
    cores = 2 if n_ph % 2 == 0 else 1
    n_z = n_ph // cores
    el_place = lax.axis_index("el")
    ph_place = lax.axis_index("ph")
    z_place, core_place = ph_place // cores, ph_place % cores

    live = jnp.arange(slots, dtype=jnp.int32) < tile_count[0, 0]
    row_ids, col_ids = tile_rows[0, 0], tile_cols[0, 0]
    col_owner = col_ids // phon_span
    row_owner = row_ids // elec_span
    row_z, row_core = row_owner // cores, row_owner % cores
    if n_el & (n_el - 1) == 0:
        phon_in = phon_out = col_owner ^ el_place
    else:
        phon_in, phon_out = (el_place - col_owner) % n_el, (col_owner - el_place) % n_el
    if n_z & (n_z - 1) == 0:
        elec_in = elec_out = row_z ^ z_place
    else:
        elec_in, elec_out = (z_place - row_z) % n_z, (row_z - z_place) % n_z
    other_core = (row_core != core_place).astype(jnp.int32)
    phon_in = phon_in * phon_span + col_ids % phon_span
    phon_out = phon_out * phon_span + col_ids % phon_span
    elec_in = (other_core * n_z + elec_in) * elec_span + row_ids % elec_span
    elec_out = (other_core * n_z + elec_out) * elec_span + row_ids % elec_span
    phon_out = jnp.where(live, phon_out, phon_blocks)
    elec_out = jnp.where(live, elec_out, elec_blocks)
    group_count = (tile_count[0] + (group - 1)) // group

    def after(values, first):
        return list(lax.optimization_barrier((list(values), list(first)))[0])

    def over_el(values):
        return [
            send(value, "el", n_el, partner(n_el, step + 1)) for step, value in enumerate(values)
        ]

    def over_z(values):
        def place_of(step):
            z_of = partner(n_z, step)
            return lambda place: z_of(place // cores) * cores + place % cores

        return [send(value, "ph", n_ph, place_of(step + 1)) for step, value in enumerate(values)]

    def over_core(value):
        return send(value, "ph", n_ph, lambda place: place ^ 1)

    def spread_phon(value):
        half = phon_span // 2
        if RELAY and n_el == 4 and half:
            near, far = over_el([value] * 2)
            halves = split(near, far, half)
            passed = [
                send(piece, "el", n_el, partner(n_el, step + 1)) for step, piece in enumerate(halves)
            ]
            return [value, near, far, *passed], halves
        pieces = [value] + over_el([value] * (n_el - 1))
        return pieces, pieces[1:2]

    def spread_elec(value, first):
        same_core = [value] + over_z([value] * (n_z - 1))
        if cores == 1:
            return same_core
        others = after(same_core[1:], first)
        return same_core + [over_core(piece) for piece in [value] + others]

    elec_terms = [[(step, index) for step in range(n_z - 1)] for index in range(elec_span)]
    half = phon_span // 2
    relay = RELAY and n_el == 4 and phon_span % 2 == 0
    near, far, both = phon_span, 2 * phon_span, 3 * phon_span
    if relay:
        plan = [
            [start + index for start in (both, near) for index in range(half)],
            [start + index for start in (both, far) for index in range(half, phon_span)],
        ]
        combined = [list(range(half)), list(range(half, phon_span))]
        phon_terms = [[(0, half + index), (3, index)] for index in range(half)]
        phon_terms += [[(1, half + index), (2, index)] for index in range(half)]
    else:
        plan = [
            list(range((step + 1) * phon_span, (step + 2) * phon_span)) for step in range(n_el - 1)
        ]
        phon_terms = [[(step, index) for step in range(n_el - 1)] for index in range(phon_span)]
    middle = elec_blocks // 2
    kept = (
        [(0, middle), (middle, elec_blocks)],
        [(0, phon_span)] + [(near + half, far + half)] * relay,
        plan,
    )
    ids = (elec_in, elec_out, phon_in, phon_out, group_count)
    elec_now, phon_now = elec_dev.astype(jnp.bfloat16), phon_dev[0].astype(jnp.bfloat16)
    for sweep in range(ITERS):
        dtype = jnp.bfloat16 if sweep + 1 < ITERS else jnp.float32
        phon_pieces, passed = spread_phon(phon_now)
        elec_pieces = spread_elec(elec_now, passed)
        (elec_own, given), phon_own, phon_coded = drags(
            ids, tile_set, group, elec_pieces, phon_pieces, kept
        )
        theirs = over_core(given)
        elec_own, *elec_coded = pair_sum(elec_own, theirs, n_z - 1)
        elec_coded = over_z(elec_coded)
        phon_coded = over_el(phon_coded)
        if relay:
            taken = after(phon_coded[::-1], [elec_own, *elec_coded[:EARLY]])
            phon_coded += over_el(combine(phon_own[1], taken, combined))
        (phon_kept,) = after(phon_own[:1], [elec_own, *elec_coded[:TIES]])
        phon_now = renew(phon_source[0], phon_kept, phon_coded, phon_terms, phon_rate[0], dtype)
        (elec_own,) = after([elec_own], [phon_now])
        elec_now = renew(elec_source, elec_own, elec_coded, elec_terms, elec_rate, dtype)
    return (elec_now, phon_now[None])


def solution(mesh):
    in_specs = (
        P(("el", "ph"), None, None),
        P("ph", "el", None, None),
        P(("el", "ph"), None, None),
        P("ph", "el", None, None),
        P(("el", "ph"), None),
        P("ph", "el", None),
        P("el", "ph", None, None, None),
        P("el", "ph", None),
        P("el", "ph", None),
        P("el", "ph"),
    )
    out_specs = (P(("el", "ph"), None, None), P("ph", "el", None, None))
    body = functools.partial(local, mesh.shape["el"], mesh.shape["ph"])
    return jax.shard_map(body, mesh=mesh, in_specs=in_specs, out_specs=out_specs, check_vma=False)
```
